512 devices in a mesh: gx: 16 (over x_hi, y, core), gy: 32 (over x_lo, z).
Axes of the slice: x: 4 (x_hi: 2, x_lo: 2; x = x_hi * 2 + x_lo), y: 4, z: 16, core: 2. Of those that a mesh axis runs over, the one named last changes fastest.
Arguments:
- matrix: bfloat16 [2097152, 256], P(('gx', 'gy')), as said below
- pattern: int32 [16384, 2], P(('gx', 'gy')), may hold values 0 or 1
Outputs:
- basis: bfloat16 [2097152, 256], P(('gx', 'gy'))
- upper: float32 [256, 256], replicated
The draws below stay inside these ranges and needn't reach their ends.
Inputs may be any that keep to these rules, and one draw needn't show every extreme that they name: matrix has full column rank after masking, with columns of unlike scales.
All inputs are finite; a program needn't handle non-finite values. No bound on the sum of `pattern` on one device may be relied on, other than what follows from the above.
Results may differ from the reference program's by a relative error of at most 0.001.
Values sent between devices are 32-bit elements; how exact they have to be, the bound alone decides.
A program may use at most 64 MiB of HBM per device.

```python
import jax
import jax.numpy as jnp
from jax import lax

NB = 256
BLOCK = 128
ROWS_DEV = 4096
ROWS = 2097152


def draw_matrix(key, part):
    key = jax.random.fold_in(key, 11)
    keys = jax.random.split(key, 5)
    devices_all = ROWS // ROWS_DEV
    noise = jax.random.normal(keys[0], (ROWS, NB), jnp.float32)
    owner = jnp.arange(ROWS, dtype=jnp.int32) // ROWS_DEV
    position = owner.astype(jnp.float32) / jnp.float32(max(devices_all - 1, 1))
    rising = (1.0 + 2.0 * position)[:, None]
    order = jax.random.permutation(keys[2], NB)
    column = order[owner % NB]
    onehot = (column[:, None] == jnp.arange(NB, dtype=jnp.int32)[None, :]).astype(jnp.float32)
    spike = 8.0 * onehot * jax.random.normal(keys[3], (ROWS, NB), jnp.float32)
    colscale = jnp.exp(jax.random.uniform(keys[4], (1, NB), jnp.float32) * jnp.log(10.0))
    rowscale = jnp.exp(jax.random.uniform(keys[1], (ROWS, 1), jnp.float32) * jnp.log(3.0))
    values = noise * rowscale * rising * colscale + spike
    return values.astype(jnp.bfloat16)


def plant(result, own_key, low, largest):
    extent = result.shape
    spot = [jax.random.randint(jax.random.fold_in(own_key, axis), (), 0, extent[axis]) for axis in range(len(extent))]
    result = result.at[tuple(spot)].set(low)
    longest = extent.index(max(extent))
    spot[longest] = (spot[longest] + 1) % extent[longest]
    return result.at[tuple(spot)].set(largest)


def setup_inputs(seed: int = 0) -> dict:
    key_list = jax.random.split(jax.random.key(seed), 3)
    return {
        "matrix": draw_matrix(jax.random.fold_in(key_list[2], 71), 0),
        "pattern": plant((jax.random.randint(key_list[1], (ROWS // BLOCK, NB // BLOCK), 0, 4) < 3).astype(jnp.int32), jax.random.fold_in(key_list[1], 1), 0, 1),
    }


def factor_gram(gram):
    count = gram.shape[0]
    column_ids = jnp.arange(count, dtype=jnp.int32)

    def one_pivot(step, carry):
        remain, upper = carry
        index = jnp.asarray(step).astype(jnp.int32)
        row = lax.dynamic_slice_in_dim(remain, index, 1, 0)[0]
        pivot = lax.dynamic_slice_in_dim(row, index, 1, 0)[0]
        row = jnp.where(column_ids >= index, row / jnp.sqrt(pivot), jnp.zeros_like(row))
        upper = lax.dynamic_update_slice_in_dim(upper, row[None, :], index, 0)
        remain = remain - row[:, None] * row[None, :]
        return (remain, upper)
    _, upper = lax.fori_loop(0, count, one_pivot, (gram, jnp.zeros_like(gram)))
    return upper

def invert_upper(upper):
    count = upper.shape[0]
    column_ids = jnp.arange(count, dtype=jnp.int32)

    def one_row(step, inverse):
        index = (count - 1 - jnp.asarray(step)).astype(jnp.int32)
        row = lax.dynamic_slice_in_dim(upper, index, 1, 0)[0]
        pivot = lax.dynamic_slice_in_dim(row, index, 1, 0)[0]
        unit = (column_ids == index).astype(upper.dtype)
        solved = (unit - jnp.dot(row, inverse, precision=lax.Precision.HIGHEST)) / pivot
        return lax.dynamic_update_slice_in_dim(inverse, solved[None, :], index, 0)
    return lax.fori_loop(0, count, one_row, jnp.zeros_like(upper))

def reference(matrix, pattern):
    blocks = matrix.reshape(ROWS // BLOCK, BLOCK, NB // BLOCK, BLOCK)
    keep = pattern.astype(jnp.bfloat16)
    masked = (blocks * keep[:, None, :, None]).reshape(ROWS, NB)
    gram = lax.dot_general(masked, masked, (((0,), (0,)), ((), ())), preferred_element_type=jnp.float32)
    gram = gram / jnp.float32(ROWS)
    upper = factor_gram(gram)
    inverse = invert_upper(upper)
    pieces = masked.reshape(ROWS // ROWS_DEV, ROWS_DEV, NB)

    def one_piece(piece):
        return jnp.dot(piece.astype(jnp.float32), inverse, precision=lax.Precision.HIGHEST).astype(jnp.bfloat16)
    basis = lax.map(one_piece, pieces).reshape(ROWS, NB)
    return (basis, upper)
```

```python
import functools

import jax
import jax.numpy as jnp
from jax import lax
from jax.experimental import pallas as pl
from jax.experimental.pallas import tpu as pltpu
from jax.sharding import PartitionSpec as P

BLOCK = 128
NB = 256
F32 = jnp.float32
BF16 = jnp.bfloat16
HIGHEST = lax.Precision.HIGHEST
MESH = pl.DeviceIdType.MESH

NX, NY, NZ, NC = 4, 4, 16, 2
PLANE = NX * NY * NC
PIECE = 9


def ring(step, size):
    return min(step, size - step)


PLANE_STEPS = sorted(
    ((dx, dy, dc) for dx in range(NX) for dy in range(NY) for dc in range(NC) if dx or dy or dc),
    key=lambda s: -(ring(s[0], NX) + ring(s[1], NY) + 0.5 * s[2]),
)
Z_STEPS = sorted(range(1, NZ), key=lambda s: -ring(s, NZ))


def place():
    gx, gy = lax.axis_index("gx"), lax.axis_index("gy")
    x = gx // (NY * NC) * 2 + gy // NZ
    return x, gx // NC % NY, gy % NZ, gx % NC


def device(x, y, z, core):
    return (x // 2 * NY + y) * NC + core, x % 2 * NZ + z


def gram_kernel(chunks, matrix, pattern, out, held, send, recv, zbuf, final,
                in_sems, rs_send, rs_recv, z_send, z_recv, ag_send, ag_recv):
    rows = held.shape[0]
    step = rows // chunks
    loads = []
    for i in range(chunks):
        part = pl.ds(i * step, step)
        load = pltpu.make_async_copy(matrix.at[part], held.at[part], in_sems.at[i])
        load.start()
        loads.append(load)

    x, y, z, core = place()
    mine = (x * NY + y) * NC + core
    plane = []
    for dx, dy, dc in PLANE_STEPS:
        px, py, pc = (x + dx) % NX, (y + dy) % NY, (core + dc) % NC
        plane.append((device(px, py, z, pc), (px * NY + py) * NC + pc))
    line = [device(x, y, (z + dz) % NZ, core) for dz in Z_STEPS]

    barrier = pltpu.get_barrier_semaphore()
    for where, _ in plane:
        pl.semaphore_signal(barrier, inc=1, device_id=where, device_id_type=MESH)
    for where in line:
        pl.semaphore_signal(barrier, inc=1, device_id=where, device_id_type=MESH)

    gram = jnp.zeros((NB, NB), F32)
    for i in range(chunks):
        loads[i].wait()
        blocks = []
        for b in range(step // BLOCK):
            at = i * step + b * BLOCK
            halves = []
            for h in range(NB // BLOCK):
                keep = pattern[at // BLOCK, h] != 0
                halves.append(jnp.where(keep, held[at : at + BLOCK, h * BLOCK : h * BLOCK + BLOCK], 0).astype(BF16))
            blocks.append(jnp.concatenate(halves, axis=1))
        masked = jnp.concatenate(blocks, axis=0)
        gram += lax.dot_general(masked, masked, (((0,), (0,)), ((), ())), preferred_element_type=F32)

    r = lax.broadcasted_iota(jnp.int32, (BLOCK, BLOCK), 0)
    c = lax.broadcasted_iota(jnp.int32, (BLOCK, BLOCK), 1)
    g00, g01, g11 = gram[:BLOCK, :BLOCK], gram[:BLOCK, BLOCK:], gram[BLOCK:, BLOCK:]
    both = jnp.where(c >= r, g00, g11)
    diagonal = jnp.sum(jnp.where(c == r, g11, 0.0), axis=0, keepdims=True)
    send[: PLANE // 2, :8, :] = g01.reshape(PLANE // 2, 8, BLOCK)
    send[PLANE // 2 :, :8, :] = both.reshape(PLANE // 2, 8, BLOCK)
    send[:, 8:, :] = jnp.broadcast_to(diagonal[None], (PLANE, 1, BLOCK))

    pl.semaphore_wait(barrier, len(plane) + len(line))

    copies = []
    for n, (where, piece) in enumerate(plane):
        copy = pltpu.make_async_remote_copy(
            src_ref=send.at[piece], dst_ref=recv.at[n], send_sem=rs_send.at[n], recv_sem=rs_recv.at[n],
            device_id=where, device_id_type=MESH)
        copy.start()
        copies.append(copy)
    for copy in copies:
        copy.wait_recv()
    total = send[mine]
    for n in range(len(plane)):
        total += recv[n]
    zbuf[z] = total

    zcopies = []
    for n, where in enumerate(line):
        copy = pltpu.make_async_remote_copy(
            src_ref=zbuf.at[z], dst_ref=zbuf.at[z], send_sem=z_send.at[n], recv_sem=z_recv.at[z],
            device_id=where, device_id_type=MESH)
        copy.start()
        zcopies.append(copy)
    for dz in Z_STEPS:
        other = (z + dz) % NZ
        pltpu.make_async_remote_copy(
            src_ref=zbuf.at[other], dst_ref=zbuf.at[other], send_sem=z_send.at[0], recv_sem=z_recv.at[other],
            device_id=line[0], device_id_type=MESH).wait_recv()
    total = zbuf[0]
    for n in range(1, NZ):
        total += zbuf[n]
    final[mine] = total

    acopies = []
    for n, (where, _) in enumerate(plane):
        copy = pltpu.make_async_remote_copy(
            src_ref=final.at[mine], dst_ref=final.at[mine], send_sem=ag_send.at[n], recv_sem=ag_recv.at[mine],
            device_id=where, device_id_type=MESH)
        copy.start()
        acopies.append(copy)
    for where, piece in plane:
        pltpu.make_async_remote_copy(
            src_ref=final.at[piece], dst_ref=final.at[piece], send_sem=ag_send.at[0], recv_sem=ag_recv.at[piece],
            device_id=where, device_id_type=MESH).wait_recv()
    out[...] = final[...]
    for copy in copies + zcopies + acopies:
        copy.wait_send()


def summed_gram(matrix, pattern, chunks=4):
    rows = matrix.shape[0]
    piece = (PIECE, BLOCK)
    dma = pltpu.SemaphoreType.DMA
    return pl.pallas_call(
        functools.partial(gram_kernel, chunks),
        out_shape=jax.ShapeDtypeStruct((PLANE,) + piece, F32),
        in_specs=[pl.BlockSpec(memory_space=pl.ANY), pl.BlockSpec(memory_space=pltpu.SMEM)],
        out_specs=pl.BlockSpec(memory_space=pltpu.VMEM),
        scratch_shapes=[
            pltpu.VMEM((rows, NB), BF16),
            pltpu.VMEM((PLANE,) + piece, F32),
            pltpu.VMEM((PLANE - 1,) + piece, F32),
            pltpu.VMEM((NZ,) + piece, F32),
            pltpu.VMEM((PLANE,) + piece, F32),
            dma((chunks,)),
            dma((PLANE - 1,)), dma((PLANE - 1,)),
            dma((NZ - 1,)), dma((NZ,)),
            dma((PLANE - 1,)), dma((PLANE,)),
        ],
        compiler_params=pltpu.CompilerParams(collective_id=0, has_side_effects=True, vmem_limit_bytes=24 << 20),
        cost_estimate=pl.CostEstimate(flops=2 * rows * NB * NB, bytes_accessed=2 * rows * NB, transcendentals=0),
        name="gram_sum",
    )(matrix, pattern)


def eliminate(panel, block):
    size = block.shape[0]
    tiles, lanes = size // 8, panel.shape[1] // 128
    cols = [jnp.broadcast_to(block[k // 8 * 8 :, k : k + 1], (size - k // 8 * 8, 128)) for k in range(size)]
    parts = [[panel[8 * t : 8 * t + 8, 128 * c : 128 * c + 128] for c in range(lanes)] for t in range(tiles)]
    sub = lax.broadcasted_iota(jnp.int32, (8, 128), 0)
    pivots = []
    for j in range(size):
        t0, s = j // 8, j % 8
        col = cols[j]
        pivot = jnp.broadcast_to(col[s : s + 1], (8, 128))
        inverse = 1.0 / pivot
        seen = pivot if s == 0 else jnp.where(sub >= s, pivot, seen)
        if s == 7:
            pivots.append(seen)
        for k in range(j + 1, size):
            first = k // 8 - t0
            row = col[k - 8 * t0 : k - 8 * t0 + 1] * inverse[0:1]
            cols[k] = cols[k] - col[8 * first :] * jnp.broadcast_to(row, (size - k // 8 * 8, 128))
        for t in range(t0, tiles):
            scaled = col[8 * (t - t0) : 8 * (t - t0) + 8] * inverse
            if t == t0:
                if s == 7:
                    continue
                scaled = jnp.where(sub > s, scaled, 0.0)
            for c in range(lanes):
                parts[t][c] = parts[t][c] - scaled * jnp.broadcast_to(parts[t0][c][s : s + 1], (8, 128))
    rows = []
    for t in range(tiles):
        scale = lax.rsqrt(pivots[t])
        rows.append(jnp.concatenate([p * scale for p in parts[t]], axis=1))
    return jnp.concatenate(rows, axis=0)


def factor(work, size):
    n = work.shape[0]
    for r0 in range(0, n, size):
        r1 = r0 + size
        low, high = r0 // 128 * 128, n + (r1 + 127) // 128 * 128
        panel = work[r0:r1, low:high]
        rows = eliminate(panel, panel[:, r0 - low : r1 - low])
        work[r0:r1, low:high] = rows
        cut = r1 // 128 * 128
        for a, e in ((r1, r1 + size), (r1 + size, n)):
            if a < e <= n:
                work[a:e, cut:high] = work[a:e, cut:high] - lax.dot_general(
                    rows[:, a - low : e - low], rows[:, cut - low :], (((0,), (0,)), ((), ())),
                    precision=HIGHEST, preferred_element_type=F32)


def basis_kernel(chunks, total_rows, gram, matrix, pattern, basis, upper, work, held, made, in_sems, out_sems):
    rows = held.shape[0]
    step = rows // chunks
    loads = []
    for i in range(chunks):
        part = pl.ds(i * step, step)
        load = pltpu.make_async_copy(matrix.at[part], held.at[part], in_sems.at[i])
        load.start()
        loads.append(load)

    scale = 1.0 / total_rows
    g01 = gram[: PLANE // 2, :8, :].reshape(BLOCK, BLOCK) * scale
    both = gram[PLANE // 2 :, :8, :].reshape(BLOCK, BLOCK) * scale
    diagonal = gram[0, 8:, :] * scale
    flipped = both.T
    r = lax.broadcasted_iota(jnp.int32, (BLOCK, BLOCK), 0)
    c = lax.broadcasted_iota(jnp.int32, (BLOCK, BLOCK), 1)
    unit = jnp.where(r == c, 1.0, 0.0)
    zero = jnp.zeros((BLOCK, BLOCK), F32)
    work[:BLOCK, :BLOCK] = jnp.where(c >= r, both, flipped)
    work[:BLOCK, BLOCK:NB] = g01
    work[BLOCK:, BLOCK:NB] = jnp.where(c < r, both, jnp.where(c > r, flipped, diagonal))
    work[:BLOCK, NB : NB + BLOCK] = unit
    work[:BLOCK, NB + BLOCK :] = zero
    work[BLOCK:, NB : NB + BLOCK] = zero
    work[BLOCK:, NB + BLOCK :] = unit
    factor(work, 32)
    r = lax.broadcasted_iota(jnp.int32, (NB, NB), 0)
    c = lax.broadcasted_iota(jnp.int32, (NB, NB), 1)
    upper[...] = jnp.where(c >= r, work[:, :NB], 0.0)
    inverse = jnp.where(c <= r, work[:, NB:], 0.0)
    head = inverse.astype(BF16)
    tail = (inverse - head.astype(F32)).astype(BF16)

    stores = []
    for i in range(chunks):
        loads[i].wait()
        blocks = []
        for b in range(step // BLOCK):
            at = i * step + b * BLOCK
            halves = []
            for h in range(NB // BLOCK):
                keep = pattern[at // BLOCK, h] != 0
                halves.append(jnp.where(keep, held[at : at + BLOCK, h * BLOCK : h * BLOCK + BLOCK], 0).astype(BF16))
            blocks.append(jnp.concatenate(halves, axis=1))
        masked = jnp.concatenate(blocks, axis=0)
        dims = (((1,), (1,)), ((), ()))
        result = lax.dot_general(masked, head, dims, preferred_element_type=F32)
        result += lax.dot_general(masked, tail, dims, preferred_element_type=F32)
        part = pl.ds(i * step, step)
        made[part, :] = result.astype(BF16)
        store = pltpu.make_async_copy(made.at[part], basis.at[part], out_sems.at[i])
        store.start()
        stores.append(store)
    for store in stores:
        store.wait()


def factor_and_basis(gram, matrix, pattern, total_rows, chunks=8):
    rows = matrix.shape[0]
    vmem = pl.BlockSpec(memory_space=pltpu.VMEM)
    hbm = pl.BlockSpec(memory_space=pl.ANY)
    return pl.pallas_call(
        functools.partial(basis_kernel, chunks, float(total_rows)),
        out_shape=(jax.ShapeDtypeStruct((rows, NB), BF16), jax.ShapeDtypeStruct((NB, NB), F32)),
        in_specs=[vmem, hbm, pl.BlockSpec(memory_space=pltpu.SMEM)],
        out_specs=(hbm, vmem),
        scratch_shapes=[
            pltpu.VMEM((NB, 2 * NB), F32),
            pltpu.VMEM((rows, NB), BF16),
            pltpu.VMEM((rows, NB), BF16),
            pltpu.SemaphoreType.DMA((chunks,)),
            pltpu.SemaphoreType.DMA((chunks,)),
        ],
        compiler_params=pltpu.CompilerParams(vmem_limit_bytes=24 << 20),
        cost_estimate=pl.CostEstimate(flops=4 * rows * NB * NB, bytes_accessed=4 * rows * NB, transcendentals=0),
        name="factor_basis",
    )(gram, matrix, pattern)


def local(matrix, pattern):
    total_rows = matrix.shape[0] * lax.axis_size("gx") * lax.axis_size("gy")
    gram = summed_gram(matrix, pattern)
    return factor_and_basis(gram, matrix, pattern, total_rows)


def solution(mesh):
    placed = (P(("gx", "gy"), None), P(("gx", "gy"), None))
    return jax.shard_map(
        local, mesh=mesh, in_specs=placed, out_specs=(P(("gx", "gy"), None), P()), check_vma=False
    )
```

```python
import functools

import jax
import jax.numpy as jnp
from jax import lax
from jax.experimental import pallas as pl
from jax.experimental.pallas import tpu as pltpu
from jax.sharding import PartitionSpec as P

BLOCK = 128
NB = 256
F32 = jnp.float32
BF16 = jnp.bfloat16
MESH = pl.DeviceIdType.MESH

NX, NY, NZ, NC = 4, 4, 16, 2
PLANE = NX * NY * NC
PIECE = 9


def ring(step, size):
    return min(step, size - step)


PLANE_STEPS = sorted(
    ((dx, dy, dc) for dx in range(NX) for dy in range(NY) for dc in range(NC) if dx or dy or dc),
    key=lambda s: -(ring(s[0], NX) + ring(s[1], NY) + 0.5 * s[2]),
)
Z_STEPS = sorted(range(1, NZ), key=lambda s: -ring(s, NZ))
Z_NEAR = [s for s in Z_STEPS if ring(s, NZ) <= 4]


def place():
    gx, gy = lax.axis_index("gx"), lax.axis_index("gy")
    x = gx // (NY * NC) * 2 + gy // NZ
    return x, gx // NC % NY, gy % NZ, gx % NC


def device(x, y, z, core):
    return (x // 2 * NY + y) * NC + core, x % 2 * NZ + z


def gram_kernel(chunks, matrix, pattern, out, masked, keeps, send, recv, zbuf, final,
                in_sems, keep_sem, rs_send, rs_recv, z_send, z_recv, ag_send, ag_recv, far_sem):
    rows = masked.shape[0]
    step = rows // chunks
    x, y, z, core = place()
    mine = (x * NY + y) * NC + core
    plane = []
    for dx, dy, dc in PLANE_STEPS:
        px, py, pc = (x + dx) % NX, (y + dy) % NY, (core + dc) % NC
        plane.append((device(px, py, z, pc), (px * NY + py) * NC + pc))
    line = {dz: device(x, y, (z + dz) % NZ, core) for dz in Z_STEPS}

    barrier = pltpu.get_barrier_semaphore()
    for where, _ in plane:
        pl.semaphore_signal(barrier, inc=1, device_id=where, device_id_type=MESH)
    for dz in Z_NEAR:
        pl.semaphore_signal(barrier, inc=1, device_id=line[dz], device_id_type=MESH)

    keep_load = pltpu.make_async_copy(pattern, keeps, keep_sem)
    keep_load.start()
    loads = []
    for i in range(chunks):
        part = pl.ds(i * step, step)
        load = pltpu.make_async_copy(matrix.at[part], masked.at[part], in_sems.at[i])
        load.start()
        loads.append(load)

    keep_load.wait()
    gram = jnp.zeros((NB, NB), F32)
    for i in range(chunks):
        loads[i].wait()
        for at in range(i * step, i * step + step, BLOCK):
            for h in range(NB // BLOCK):
                block = (slice(at, at + BLOCK), slice(h * BLOCK, h * BLOCK + BLOCK))
                masked[block] = jnp.where(keeps[h, at // BLOCK] != 0, masked[block], 0).astype(BF16)
        part = masked[i * step : i * step + step, :]
        gram += lax.dot_general(part, part, (((0,), (0,)), ((), ())), preferred_element_type=F32)

    r = lax.broadcasted_iota(jnp.int32, (BLOCK, BLOCK), 0)
    c = lax.broadcasted_iota(jnp.int32, (BLOCK, BLOCK), 1)
    g00, g01, g11 = gram[:BLOCK, :BLOCK], gram[:BLOCK, BLOCK:], gram[BLOCK:, BLOCK:]
    both = jnp.where(c >= r, g00, g11)
    diagonal = jnp.sum(jnp.where(c == r, g11, 0.0), axis=0, keepdims=True)
    send[: PLANE // 2, :8, :] = g01.reshape(PLANE // 2, 8, BLOCK)
    send[PLANE // 2 :, :8, :] = both.reshape(PLANE // 2, 8, BLOCK)
    send[:, 8:, :] = jnp.broadcast_to(diagonal[None], (PLANE, 1, BLOCK))

    pl.semaphore_wait(barrier, len(plane) + len(Z_NEAR))

    copies = []
    for n, (where, piece) in enumerate(plane):
        copy = pltpu.make_async_remote_copy(
            src_ref=send.at[piece], dst_ref=recv.at[n], send_sem=rs_send.at[n], recv_sem=rs_recv.at[n],
            device_id=where, device_id_type=MESH)
        copy.start()
        copies.append(copy)
    for dz in (4, NZ - 4):
        pl.semaphore_signal(far_sem, inc=1, device_id=line[dz], device_id_type=MESH)
    for copy in copies:
        copy.wait_recv()
    total = send[mine]
    for n in range(len(plane)):
        total += recv[n]
    zbuf[z] = total
    pl.semaphore_wait(far_sem, 2)

    zcopies = []
    for n, dz in enumerate(Z_STEPS):
        copy = pltpu.make_async_remote_copy(
            src_ref=zbuf.at[z], dst_ref=zbuf.at[z], send_sem=z_send.at[n], recv_sem=z_recv.at[z],
            device_id=line[dz], device_id_type=MESH)
        copy.start()
        zcopies.append(copy)
    for dz in Z_STEPS:
        other = (z + dz) % NZ
        pltpu.make_async_remote_copy(
            src_ref=zbuf.at[other], dst_ref=zbuf.at[other], send_sem=z_send.at[0], recv_sem=z_recv.at[other],
            device_id=line[dz], device_id_type=MESH).wait_recv()
    total = zbuf[0]
    for n in range(1, NZ):
        total += zbuf[n]
    final[mine] = total

    acopies = []
    for n, (where, _) in enumerate(plane):
        copy = pltpu.make_async_remote_copy(
            src_ref=final.at[mine], dst_ref=final.at[mine], send_sem=ag_send.at[n], recv_sem=ag_recv.at[mine],
            device_id=where, device_id_type=MESH)
        copy.start()
        acopies.append(copy)
    for where, piece in plane:
        pltpu.make_async_remote_copy(
            src_ref=final.at[piece], dst_ref=final.at[piece], send_sem=ag_send.at[0], recv_sem=ag_recv.at[piece],
            device_id=where, device_id_type=MESH).wait_recv()
    out[...] = final[...]
    for copy in copies + zcopies + acopies:
        copy.wait_send()


def summed_gram(matrix, pattern, chunks=4):
    rows = matrix.shape[0]
    piece = (PIECE, BLOCK)
    dma = pltpu.SemaphoreType.DMA
    hbm = pl.BlockSpec(memory_space=pltpu.HBM)
    vmem = pl.BlockSpec(memory_space=pltpu.VMEM)
    return pl.pallas_call(
        functools.partial(gram_kernel, chunks),
        out_shape=(jax.ShapeDtypeStruct((PLANE,) + piece, F32), jax.ShapeDtypeStruct((rows, NB), BF16)),
        in_specs=[hbm, hbm],
        out_specs=(vmem, vmem),
        scratch_shapes=[
            pltpu.SMEM(pattern.shape, jnp.int32),
            pltpu.VMEM((PLANE,) + piece, F32),
            pltpu.VMEM((PLANE - 1,) + piece, F32),
            pltpu.VMEM((NZ,) + piece, F32),
            pltpu.VMEM((PLANE,) + piece, F32),
            dma((chunks,)), dma,
            dma((PLANE - 1,)), dma((PLANE - 1,)),
            dma((NZ - 1,)), dma((NZ,)),
            dma((PLANE - 1,)), dma((PLANE,)),
            pltpu.SemaphoreType.REGULAR,
        ],
        compiler_params=pltpu.CompilerParams(collective_id=0, has_side_effects=True, vmem_limit_bytes=24 << 20),
        cost_estimate=pl.CostEstimate(flops=2 * rows * NB * NB, bytes_accessed=2 * rows * NB, transcendentals=0),
        name="gram_sum",
    )(matrix, pattern)


def eliminate(panel, at, size, group, tick):
    tiles, lanes = size // 8, panel.shape[1] // 128
    tile = (8, 128)
    parts = [[panel[8 * t : 8 * t + 8, 128 * c : 128 * c + 128] for c in range(lanes)] for t in range(tiles)]
    sub = lax.broadcasted_iota(jnp.int32, tile, 0)
    pivots = [None] * tiles
    for q in range(0, size, group):
        cols = []
        for k in range(q, q + group):
            c, lane = divmod(at + k, 128)
            cols.append([
                jnp.broadcast_to(parts[t][c][:, lane : lane + 1], tile) if t >= k // 8 else None for t in range(tiles)
            ])
        for j in range(q, q + group):
            t0, s = divmod(j, 8)
            col = cols[j - q]
            pivot = jnp.broadcast_to(col[t0][s : s + 1], tile)
            inverse = 1.0 / pivot
            pivots[t0] = pivot if s == 0 else jnp.where(sub >= s, pivot, pivots[t0])
            scaled = [col[t] * inverse if t >= t0 else None for t in range(tiles)]
            for k in range(j + 1, q + group):
                tk, sk = divmod(k, 8)
                row = jnp.broadcast_to(col[tk][sk : sk + 1], tile)
                for t in range(tk, tiles):
                    term = (col[t] * row) * inverse if k == j + 1 else scaled[t] * row
                    cols[k - q][t] = cols[k - q][t] - term
            heads = [jnp.broadcast_to(parts[t0][c][s : s + 1], tile) for c in range(lanes)]
            for t in range(t0, tiles):
                if t == t0 and s == 7:
                    continue
                factors = jnp.where(sub > s, scaled[t], 0.0) if t == t0 else scaled[t]
                for c in range(lanes):
                    parts[t][c] = parts[t][c] - factors * heads[c]
            tick()
    rows = []
    for t in range(tiles):
        scale = lax.rsqrt(pivots[t])
        rows.append(jnp.concatenate([p * scale for p in parts[t]], axis=1))
    return jnp.concatenate(rows, axis=0)


def split(value, terms):
    parts = []
    for _ in range(terms):
        parts.append(value.astype(BF16))
        value = value - parts[-1].astype(F32)
    return parts


def factor(work, size, group, done, tick):
    n = work.shape[0]
    for r0 in range(0, n, size):
        r1 = r0 + size
        low, high = r0 // 128 * 128, n + (r1 + 127) // 128 * 128
        rows = eliminate(work[r0:r1, low:high], r0 - low, size, group, tick)
        work[r0:r1, low:high] = rows
        cut = r1 // 128 * 128
        if r1 < n:
            h, m, l = split(rows, 3)
            left = jnp.concatenate([h, h, m, h, l, m], axis=0)
            right = jnp.concatenate([h, m, h, l, h, m], axis=0)[:, cut - low :]
            for a, e in ((r1, r1 + size), (r1 + size, n)):
                if a < e:
                    work[a:e, cut:high] = work[a:e, cut:high] - lax.dot_general(
                        left[:, a - low : e - low], right, (((0,), (0,)), ((), ())), preferred_element_type=F32)
        done(r1)


def basis_kernel(total_rows, gram, masked, basis, upper, work, triangle, made, out_sems, upper_sem):
    rows = masked.shape[0]
    pieces, chunks = rows // BLOCK, out_sems.shape[1]
    step = rows // chunks

    scale = 1.0 / total_rows
    g01 = gram[: PLANE // 2, :8, :].reshape(BLOCK, BLOCK) * scale
    both = gram[PLANE // 2 :, :8, :].reshape(BLOCK, BLOCK) * scale
    diagonal = gram[0, 8:, :] * scale
    flipped = both.T
    r = lax.broadcasted_iota(jnp.int32, (BLOCK, BLOCK), 0)
    c = lax.broadcasted_iota(jnp.int32, (BLOCK, BLOCK), 1)
    unit = jnp.where(r == c, 1.0, 0.0)
    zero = jnp.zeros((BLOCK, BLOCK), F32)
    work[:BLOCK, :BLOCK] = jnp.where(c >= r, both, flipped)
    work[:BLOCK, BLOCK:NB] = g01
    work[BLOCK:, BLOCK:NB] = jnp.where(c < r, both, jnp.where(c > r, flipped, diagonal))
    work[:BLOCK, NB : NB + BLOCK] = unit
    work[:BLOCK, NB + BLOCK :] = zero
    work[BLOCK:, NB : NB + BLOCK] = zero
    work[BLOCK:, NB + BLOCK :] = unit

    stores = []

    def send_out(i, half):
        part = (pl.ds(i * step, step), pl.ds(half * BLOCK, BLOCK))
        store = pltpu.make_async_copy(made.at[part], basis.at[part], out_sems.at[half, i])
        store.start()
        stores.append(store)

    state = {"weights": None, "ticks": 0, "next": 0}

    def first_half(i):
        rows_i = pl.ds(i * BLOCK, BLOCK)
        left = masked[rows_i, :BLOCK]
        product = jnp.dot(jnp.concatenate([left, left], axis=1), state["weights"], preferred_element_type=F32)
        made[rows_i, :BLOCK] = product.astype(BF16)
        if (i + 1) * BLOCK % step == 0:
            send_out((i + 1) * BLOCK // step - 1, 0)

    def tick():
        if state["weights"] is not None:
            state["ticks"] += 1
            while state["next"] < min(pieces, state["ticks"] * pieces // (NB - BLOCK)):
                first_half(state["next"])
                state["next"] += 1

    def done(count):
        if count == BLOCK:
            corner = jnp.where(c <= r, work[:BLOCK, NB : NB + BLOCK], 0.0).T
            state["weights"] = jnp.concatenate(split(corner, 2), axis=0)

    factor(work, 32, 16, done, tick)

    triangle[:BLOCK, :BLOCK] = jnp.where(c >= r, work[:BLOCK, :BLOCK], 0.0)
    triangle[:BLOCK, BLOCK:] = work[:BLOCK, BLOCK:NB]
    triangle[BLOCK:, :BLOCK] = zero
    triangle[BLOCK:, BLOCK:] = jnp.where(c >= r, work[BLOCK:, BLOCK:NB], 0.0)
    upper_store = pltpu.make_async_copy(triangle, upper, upper_sem)
    upper_store.start()
    stores.append(upper_store)

    corner = jnp.where(c <= r, work[BLOCK:, NB + BLOCK :], 0.0)
    columns = jnp.concatenate([work[BLOCK:, NB : NB + BLOCK].T, corner.T], axis=0)
    weights = jnp.concatenate(split(columns, 2), axis=1)
    for i in range(chunks):
        part = pl.ds(i * step, step)
        product = jnp.dot(masked[part, :], weights, preferred_element_type=F32)
        made[part, BLOCK:] = (product[:, :BLOCK] + product[:, BLOCK:]).astype(BF16)
        send_out(i, 1)
    for store in stores:
        store.wait()


def factor_and_basis(gram, masked, total_rows, chunks=8):
    rows = masked.shape[0]
    vmem = pl.BlockSpec(memory_space=pltpu.VMEM)
    hbm = pl.BlockSpec(memory_space=pltpu.HBM)
    return pl.pallas_call(
        functools.partial(basis_kernel, float(total_rows)),
        out_shape=(jax.ShapeDtypeStruct((rows, NB), BF16), jax.ShapeDtypeStruct((NB, NB), F32)),
        in_specs=[vmem, vmem],
        out_specs=(hbm, hbm),
        scratch_shapes=[
            pltpu.VMEM((NB, 2 * NB), F32),
            pltpu.VMEM((NB, NB), F32),
            pltpu.VMEM((rows, NB), BF16),
            pltpu.SemaphoreType.DMA((2, chunks)),
            pltpu.SemaphoreType.DMA,
        ],
        compiler_params=pltpu.CompilerParams(vmem_limit_bytes=24 << 20),
        cost_estimate=pl.CostEstimate(flops=4 * rows * NB * NB, bytes_accessed=4 * rows * NB, transcendentals=0),
        name="factor_basis",
    )(gram, masked)


def local(matrix, pattern):
    total_rows = matrix.shape[0] * lax.axis_size("gx") * lax.axis_size("gy")
    gram, masked = summed_gram(pltpu.with_memory_space_constraint(matrix, pltpu.HBM), pltpu.with_memory_space_constraint(pattern.T, pltpu.HBM))
    return factor_and_basis(gram, masked, total_rows)


def solution(mesh):
    placed = (P(("gx", "gy"), None), P(("gx", "gy"), None))
    return jax.shard_map(
        local, mesh=mesh, in_specs=placed, out_specs=(P(("gx", "gy"), None), P()), check_vma=False
    )
```

```python
import functools

import jax
import jax.numpy as jnp
from jax import lax
from jax.experimental import pallas as pl
from jax.experimental.pallas import tpu as pltpu
from jax.sharding import PartitionSpec as P

BLOCK = 128
NB = 256
F32 = jnp.float32
BF16 = jnp.bfloat16
MESH = pl.DeviceIdType.MESH

NX, NY, NZ, NC = 4, 4, 16, 2
PLANE = NX * NY * NC
OWNERS = ((0, 0), (1, 0), (2, 0), (3, 0), (0, 1), (0, 2), (0, 3), (1, 1))
PIECES = len(OWNERS) * NC
PIECE = NB // PIECES + 1
PASSED = ((), tuple(range(15, 9, -1)), tuple(range(3, 10)))
NEAR = len(PASSED)


def ring(step, size):
    return min(step, size - step)


def sender_order(chip):
    return -(ring(3 - chip[0], NX) + ring(3 - chip[1], NY))


PIECE_ORDER = [n * NC + core for n in sorted(range(len(OWNERS)), key=lambda n: sender_order(OWNERS[n])) for core in range(NC)]
PLANE_ORDER = sorted(
    ((x, y, core) for x in range(NX) for y in range(NY) for core in range(NC)), key=lambda s: (s[0] + s[1], s[0], s[1])
)
PLANE_STEPS = sorted(
    ((dx, dy, dc) for dx in range(NX) for dy in range(NY) for dc in range(NC) if dx or dy or dc),
    key=lambda s: -(ring(s[0], NX) + ring(s[1], NY) + 0.5 * s[2]),
)


def place():
    gx, gy = lax.axis_index("gx"), lax.axis_index("gy")
    x = gx // (NY * NC) * 2 + gy // NZ
    return x, gx // NC % NY, gy % NZ, gx % NC


def device(x, y, z, core):
    return (x // 2 * NY + y) * NC + core, x % 2 * NZ + z


def gram_kernel(chunks, matrix, pattern, out, masked, keeps, send, recv, zbuf, final,
                in_sems, keep_sem, rs_send, rs_recv, z_send, z_recv, pass_send, pass_recv, ag_send, ag_recv):
    rows = masked.shape[0]
    step = rows // chunks
    x, y, z, core = place()
    mine = (x * NY + y) * NC + core
    some_x, some_y = (x + NX - 1) // NX, (y + NY - 1) // NY
    both_one = ((NX - x) // 3) * ((NY - y) // 3)
    owner = 1 - some_x * some_y * (1 - both_one)
    piece = ((1 - some_y) * x + some_y * (3 + y + 3 * some_x)) * NC + core
    near = 1 - (z + NZ - NEAR) // NZ

    def owner_of(n):
        return OWNERS[n // NC] + (n % NC,)

    def number(spot):
        return (spot[0] * NY + spot[1]) * NC + spot[2]

    barrier = pltpu.get_barrier_semaphore()

    @pl.when(owner == 1)
    def _():
        for dx, dy, dc in PLANE_STEPS:
            where = device((x + dx) % NX, (y + dy) % NY, z, (core + dc) % NC)
            pl.semaphore_signal(barrier, inc=1, device_id=where, device_id_type=MESH)

    @pl.when(owner * near == 1)
    def _():
        for dz in range(1, NZ):
            where = device(x, y, (z + dz) % NZ, core)
            pl.semaphore_signal(barrier, inc=1, device_id=where, device_id_type=MESH)

    keep_load = pltpu.make_async_copy(pattern, keeps, keep_sem)
    keep_load.start()
    loads = []
    for i in range(chunks):
        part = pl.ds(i * step, step)
        load = pltpu.make_async_copy(matrix.at[part], masked.at[part], in_sems.at[i])
        load.start()
        loads.append(load)

    keep_load.wait()
    top, corner = jnp.zeros((BLOCK, NB), F32), jnp.zeros((BLOCK, BLOCK), F32)
    dims = (((0,), (0,)), ((), ()))
    for i in range(chunks):
        loads[i].wait()
        for at in range(i * step, i * step + step, BLOCK):
            for h in range(NB // BLOCK):
                block = (slice(at, at + BLOCK), slice(h * BLOCK, h * BLOCK + BLOCK))
                masked[block] = jnp.where(keeps[h, at // BLOCK] != 0, masked[block], 0).astype(BF16)
        part = masked[i * step : i * step + step, :]
        top += lax.dot_general(part[:, :BLOCK], part, dims, preferred_element_type=F32)
        corner += lax.dot_general(part[:, BLOCK:], part[:, BLOCK:], dims, preferred_element_type=F32)

    r = lax.broadcasted_iota(jnp.int32, (BLOCK, BLOCK), 0)
    c = lax.broadcasted_iota(jnp.int32, (BLOCK, BLOCK), 1)
    both = jnp.where(c >= r, top[:, :BLOCK], corner)
    diagonal = jnp.sum(jnp.where(c == r, corner, 0.0), axis=0, keepdims=True)
    send[: PIECES // 2, : PIECE - 1, :] = top[:, BLOCK:].reshape(PIECES // 2, PIECE - 1, BLOCK)
    send[PIECES // 2 :, : PIECE - 1, :] = both.reshape(PIECES // 2, PIECE - 1, BLOCK)
    send[:, PIECE - 1 :, :] = jnp.broadcast_to(diagonal[None], (PIECES, 1, BLOCK))

    pl.semaphore_wait(barrier, PIECES + owner * (NEAR - 1 - near))

    def to_owner(n):
        spot = owner_of(n)
        return pltpu.make_async_remote_copy(
            src_ref=send.at[n], dst_ref=recv.at[mine], send_sem=rs_send.at[n], recv_sem=rs_recv.at[mine],
            device_id=device(spot[0], spot[1], z, spot[2]), device_id_type=MESH)

    for n in PIECE_ORDER:
        pl.when(mine != number(owner_of(n)))(to_owner(n).start)

    def along_z(other, to):
        return pltpu.make_async_remote_copy(
            src_ref=zbuf.at[other], dst_ref=zbuf.at[other], send_sem=z_send.at[to], recv_sem=z_recv.at[other],
            device_id=device(x, y, to, core), device_id_type=MESH)

    def passed(to):
        return pltpu.make_async_remote_copy(
            src_ref=final.at[piece], dst_ref=final.at[piece], send_sem=pass_send.at[to], recv_sem=pass_recv,
            device_id=device(x, y, to, core), device_id_type=MESH)

    def gathered(n, spot):
        return pltpu.make_async_remote_copy(
            src_ref=final.at[n], dst_ref=final.at[n], send_sem=ag_send.at[number(spot)], recv_sem=ag_recv.at[n],
            device_id=device(spot[0], spot[1], z, spot[2]), device_id_type=MESH)

    @pl.when(owner == 1)
    def _():
        others = []
        for dx, dy, dc in PLANE_STEPS:
            others.append((((x + dx) % NX) * NY + (y + dy) % NY) * NC + (core + dc) % NC)
        for other in others:
            pltpu.make_async_remote_copy(
                src_ref=send.at[piece], dst_ref=recv.at[other], send_sem=rs_send.at[0], recv_sem=rs_recv.at[other],
                device_id=device(x, y, z, 1 - core), device_id_type=MESH).wait_recv()
        total = send[piece]
        for other in others:
            total += recv[other]
        zbuf[z] = total
        for to in range(NEAR):
            pl.when(z != to)(along_z(z, to).start)

        @pl.when(near == 1)
        def _():
            for dz in range(1, NZ):
                along_z((z + dz) % NZ, 0).wait_recv()
            total = zbuf[0]
            for n in range(1, NZ):
                total += zbuf[n]
            final[piece] = total
            for at in range(NEAR):
                if PASSED[at]:
                    @pl.when(z == at)
                    def _():
                        for to in PASSED[at]:
                            passed(to).start()

        @pl.when(near == 0)
        def _():
            passed(0).wait_recv()

        for spot in PLANE_ORDER:
            pl.when(mine != number(spot))(gathered(piece, spot).start)

    for n in range(PIECES):
        spot = owner_of(n)
        pl.when(mine != number(spot))(gathered(n, spot).wait_recv)
    out[...] = final[...]

    for n in range(PIECES):
        pl.when(mine != number(owner_of(n)))(to_owner(n).wait_send)

    @pl.when(owner == 1)
    def _():
        for to in range(NEAR):
            pl.when(z != to)(along_z(z, to).wait_send)
        for at in range(NEAR):
            if PASSED[at]:
                @pl.when(z == at)
                def _():
                    for to in PASSED[at]:
                        passed(to).wait_send()
        for spot in PLANE_ORDER:
            pl.when(mine != number(spot))(gathered(piece, spot).wait_send)


def summed_gram(matrix, pattern, chunks=2):
    rows = matrix.shape[0]
    part = (PIECE, BLOCK)
    dma = pltpu.SemaphoreType.DMA
    hbm = pl.BlockSpec(memory_space=pltpu.HBM)
    vmem = pl.BlockSpec(memory_space=pltpu.VMEM)
    return pl.pallas_call(
        functools.partial(gram_kernel, chunks),
        out_shape=(jax.ShapeDtypeStruct((PIECES,) + part, F32), jax.ShapeDtypeStruct((rows, NB), BF16)),
        in_specs=[hbm, hbm],
        out_specs=(vmem, vmem),
        scratch_shapes=[
            pltpu.SMEM(pattern.shape, jnp.int32),
            pltpu.VMEM((PIECES,) + part, F32),
            pltpu.VMEM((PLANE,) + part, F32),
            pltpu.VMEM((NZ,) + part, F32),
            pltpu.VMEM((PIECES,) + part, F32),
            dma((chunks,)), dma,
            dma((PIECES,)), dma((PLANE,)),
            dma((NEAR,)), dma((NZ,)),
            dma((NZ,)), dma,
            dma((PLANE,)), dma((PIECES,)),
        ],
        compiler_params=pltpu.CompilerParams(collective_id=0, has_side_effects=True, vmem_limit_bytes=24 << 20),
        cost_estimate=pl.CostEstimate(flops=2 * rows * NB * NB, bytes_accessed=2 * rows * NB, transcendentals=0),
        name="gram_sum",
    )(matrix, pattern)


def eliminate(panel, at, size, group, tick):
    tiles, lanes = size // 8, panel.shape[1] // 128
    tile = (8, 128)
    parts = [[panel[8 * t : 8 * t + 8, 128 * c : 128 * c + 128] for c in range(lanes)] for t in range(tiles)]
    sub = lax.broadcasted_iota(jnp.int32, tile, 0)
    pivots = [None] * tiles
    for q in range(0, size, group):
        cols = []
        for k in range(q, q + group):
            c, lane = divmod(at + k, 128)
            cols.append([
                jnp.broadcast_to(parts[t][c][:, lane : lane + 1], tile) if t >= k // 8 else None for t in range(tiles)
            ])
        for j in range(q, q + group):
            t0, s = divmod(j, 8)
            col = cols[j - q]
            pivot = jnp.broadcast_to(col[t0][s : s + 1], tile)
            inverse = 1.0 / pivot
            pivots[t0] = pivot if s == 0 else jnp.where(sub >= s, pivot, pivots[t0])
            scaled = [col[t] * inverse if t >= t0 else None for t in range(tiles)]
            for k in range(j + 1, q + group):
                tk, sk = divmod(k, 8)
                row = jnp.broadcast_to(col[tk][sk : sk + 1], tile)
                for t in range(tk, tiles):
                    term = (col[t] * row) * inverse if k == j + 1 else scaled[t] * row
                    cols[k - q][t] = cols[k - q][t] - term
            heads = [jnp.broadcast_to(parts[t0][c][s : s + 1], tile) for c in range(lanes)]
            for t in range(t0, tiles):
                if t == t0 and s == 7:
                    continue
                factors = jnp.where(sub > s, scaled[t], 0.0) if t == t0 else scaled[t]
                for c in range(lanes):
                    parts[t][c] = parts[t][c] - factors * heads[c]
            tick()
    rows = []
    for t in range(tiles):
        scale = lax.rsqrt(pivots[t])
        rows.append(jnp.concatenate([p * scale for p in parts[t]], axis=1))
    return jnp.concatenate(rows, axis=0)


def split(value, terms):
    parts = []
    for _ in range(terms):
        parts.append(value.astype(BF16))
        value = value - parts[-1].astype(F32)
    return parts


def factor(work, size, group, done, tick):
    n = work.shape[0]
    for r0 in range(0, n, size):
        r1 = r0 + size
        low, high = r0 // 128 * 128, n + (r1 + 127) // 128 * 128
        rows = eliminate(work[r0:r1, low:high], r0 - low, size, group, tick)
        work[r0:r1, low:high] = rows
        cut = r1 // 128 * 128
        if r1 < n:
            h, m, l = split(rows, 3)
            left = jnp.concatenate([h, h, m, h, l, m], axis=0)
            right = jnp.concatenate([h, m, h, l, h, m], axis=0)[:, cut - low :]
            for a, e in ((r1, r1 + size), (r1 + size, n)):
                if a < e:
                    work[a:e, cut:high] = work[a:e, cut:high] - lax.dot_general(
                        left[:, a - low : e - low], right, (((0,), (0,)), ((), ())), preferred_element_type=F32)
        done(r1)


def basis_kernel(total_rows, gram, masked, basis, upper, work, triangle, made, out_sems, upper_sem):
    rows = masked.shape[0]
    pieces, chunks = rows // BLOCK, out_sems.shape[1]
    step = rows // chunks

    scale = 1.0 / total_rows
    g01 = gram[: PIECES // 2, : PIECE - 1, :].reshape(BLOCK, BLOCK) * scale
    both = gram[PIECES // 2 :, : PIECE - 1, :].reshape(BLOCK, BLOCK) * scale
    diagonal = gram[0, PIECE - 1 :, :] * scale
    flipped = both.T
    r = lax.broadcasted_iota(jnp.int32, (BLOCK, BLOCK), 0)
    c = lax.broadcasted_iota(jnp.int32, (BLOCK, BLOCK), 1)
    unit = jnp.where(r == c, 1.0, 0.0)
    zero = jnp.zeros((BLOCK, BLOCK), F32)
    work[:BLOCK, :BLOCK] = jnp.where(c >= r, both, flipped)
    work[:BLOCK, BLOCK:NB] = g01
    work[BLOCK:, BLOCK:NB] = jnp.where(c < r, both, jnp.where(c > r, flipped, diagonal))
    work[:BLOCK, NB : NB + BLOCK] = unit
    work[:BLOCK, NB + BLOCK :] = zero
    work[BLOCK:, NB : NB + BLOCK] = zero
    work[BLOCK:, NB + BLOCK :] = unit

    stores = []

    def send_out(i, half):
        part = (pl.ds(i * step, step), pl.ds(half * BLOCK, BLOCK))
        store = pltpu.make_async_copy(made.at[part], basis.at[part], out_sems.at[half, i])
        store.start()
        stores.append(store)

    state = {"weights": None, "ticks": 0, "next": 0}

    def first_half(i):
        rows_i = pl.ds(i * BLOCK, BLOCK)
        left = masked[rows_i, :BLOCK]
        product = jnp.dot(jnp.concatenate([left, left], axis=1), state["weights"], preferred_element_type=F32)
        made[rows_i, :BLOCK] = product.astype(BF16)
        if (i + 1) * BLOCK % step == 0:
            send_out((i + 1) * BLOCK // step - 1, 0)

    def tick():
        if state["weights"] is not None:
            state["ticks"] += 1
            while state["next"] < min(pieces, state["ticks"] * pieces // (NB - BLOCK)):
                first_half(state["next"])
                state["next"] += 1

    def done(count):
        if count == BLOCK:
            corner = jnp.where(c <= r, work[:BLOCK, NB : NB + BLOCK], 0.0).T
            state["weights"] = jnp.concatenate(split(corner, 2), axis=0)

    factor(work, 32, 16, done, tick)

    triangle[:BLOCK, :BLOCK] = jnp.where(c >= r, work[:BLOCK, :BLOCK], 0.0)
    triangle[:BLOCK, BLOCK:] = work[:BLOCK, BLOCK:NB]
    triangle[BLOCK:, :BLOCK] = zero
    triangle[BLOCK:, BLOCK:] = jnp.where(c >= r, work[BLOCK:, BLOCK:NB], 0.0)
    upper_store = pltpu.make_async_copy(triangle, upper, upper_sem)
    upper_store.start()
    stores.append(upper_store)

    corner = jnp.where(c <= r, work[BLOCK:, NB + BLOCK :], 0.0)
    columns = jnp.concatenate([work[BLOCK:, NB : NB + BLOCK].T, corner.T], axis=0)
    weights = jnp.concatenate(split(columns, 2), axis=1)
    for i in range(chunks):
        part = pl.ds(i * step, step)
        product = jnp.dot(masked[part, :], weights, preferred_element_type=F32)
        made[part, BLOCK:] = (product[:, :BLOCK] + product[:, BLOCK:]).astype(BF16)
        send_out(i, 1)
    for store in stores:
        store.wait()


def factor_and_basis(gram, masked, total_rows, chunks=8):
    rows = masked.shape[0]
    vmem = pl.BlockSpec(memory_space=pltpu.VMEM)
    hbm = pl.BlockSpec(memory_space=pltpu.HBM)
    return pl.pallas_call(
        functools.partial(basis_kernel, float(total_rows)),
        out_shape=(jax.ShapeDtypeStruct((rows, NB), BF16), jax.ShapeDtypeStruct((NB, NB), F32)),
        in_specs=[vmem, vmem],
        out_specs=(hbm, hbm),
        scratch_shapes=[
            pltpu.VMEM((NB, 2 * NB), F32),
            pltpu.VMEM((NB, NB), F32),
            pltpu.VMEM((rows, NB), BF16),
            pltpu.SemaphoreType.DMA((2, chunks)),
            pltpu.SemaphoreType.DMA,
        ],
        compiler_params=pltpu.CompilerParams(vmem_limit_bytes=24 << 20),
        cost_estimate=pl.CostEstimate(flops=4 * rows * NB * NB, bytes_accessed=4 * rows * NB, transcendentals=0),
        name="factor_basis",
    )(gram, masked)


def local(matrix, pattern):
    total_rows = matrix.shape[0] * lax.axis_size("gx") * lax.axis_size("gy")
    gram, masked = summed_gram(pltpu.with_memory_space_constraint(matrix, pltpu.HBM), pltpu.with_memory_space_constraint(pattern.T, pltpu.HBM))
    return factor_and_basis(gram, masked, total_rows)


def solution(mesh):
    placed = (P(("gx", "gy"), None), P(("gx", "gy"), None))
    return jax.shard_map(
        local, mesh=mesh, in_specs=placed, out_specs=(P(("gx", "gy"), None), P()), check_vma=False
    )
```

```python
import functools

import jax
import jax.numpy as jnp
from jax import lax
from jax.experimental import pallas as pl
from jax.experimental.pallas import tpu as pltpu
from jax.sharding import PartitionSpec as P

BLOCK = 128
NB = 256
F32 = jnp.float32
BF16 = jnp.bfloat16
MESH = pl.DeviceIdType.MESH

NX, NY, NZ, NC = 4, 4, 16, 2
PLANE = NX * NY * NC
OWNERS = ((0, 0), (1, 0), (2, 0), (3, 0), (0, 1), (0, 2), (0, 3), (1, 1))
PIECES = len(OWNERS) * NC
PIECE = NB // PIECES + 1
PASSED = ((), tuple(range(15, 9, -1)), tuple(range(3, 10)))
NEAR = len(PASSED)


def ring(step, size):
    return min(step, size - step)


def sender_order(chip):
    return -(ring(3 - chip[0], NX) + ring(3 - chip[1], NY))


PIECE_ORDER = [n * NC + core for n in sorted(range(len(OWNERS)), key=lambda n: sender_order(OWNERS[n])) for core in range(NC)]
PLANE_ORDER = sorted(
    ((x, y, core) for x in range(NX) for y in range(NY) for core in range(NC)), key=lambda s: (s[0] + s[1], s[0], s[1])
)
PLANE_STEPS = sorted(
    ((dx, dy, dc) for dx in range(NX) for dy in range(NY) for dc in range(NC) if dx or dy or dc),
    key=lambda s: -(ring(s[0], NX) + ring(s[1], NY) + 0.5 * s[2]),
)


def place():
    gx, gy = lax.axis_index("gx"), lax.axis_index("gy")
    x = 2 * lax.div(gx, NY * NC) + lax.div(gy, NZ)
    return x, lax.rem(lax.div(gx, NC), NY), lax.rem(gy, NZ), lax.rem(gx, NC)


def gram_kernel(cuts, matrix, pattern, out, masked, keeps, send, recv, zbuf, final,
                in_sems, keep_sem, rs_send, rs_recv, z_send, z_recv, pass_send, pass_recv, ag_send, ag_recv):
    loads = []
    at = 0
    for i, rows in enumerate(cuts):
        part = pl.ds(at, rows)
        load = pltpu.make_async_copy(matrix.at[part], masked.at[part], in_sems.at[i])
        load.start()
        loads.append(load)
        at += rows
    keep_load = pltpu.make_async_copy(pattern, keeps, keep_sem)
    keep_load.start()

    x, y, z, core = place()
    gx, gy = lax.axis_index("gx"), lax.axis_index("gy")
    mine = (x * NY + y) * NC + core
    some_x, some_y = lax.div(x + NX - 1, NX), lax.div(y + NY - 1, NY)
    both_one = lax.div(NX - x, 3) * lax.div(NY - y, 3)
    owner = 1 - some_x * some_y * (1 - both_one)
    piece = ((1 - some_y) * x + some_y * (3 + y + 3 * some_x)) * NC + core
    near = 1 - lax.div(z + NZ - NEAR, NZ)

    def owner_of(n):
        return OWNERS[n // NC] + (n % NC,)

    def number(spot):
        return (spot[0] * NY + spot[1]) * NC + spot[2]

    def spot_id(spot):
        return (spot[0] // 2 * NY + spot[1]) * NC + spot[2], spot[0] % 2 * NZ + z

    def plane_id(to):
        return gx, gy - z + to

    barrier = pltpu.get_barrier_semaphore()

    @pl.when(owner == 1)
    def _():
        at_x = [lax.rem(x + d, NX) for d in range(NX)]
        at_y = [lax.rem(y + d, NY) * NC for d in range(NY)]
        at_core = [core, 1 - core]
        high = [lax.div(v, 2) * (NY * NC) for v in at_x]
        low = [lax.rem(v, 2) * NZ + z for v in at_x]
        for dx, dy, dc in PLANE_STEPS:
            pl.semaphore_signal(
                barrier, inc=1, device_id=(high[dx] + at_y[dy] + at_core[dc], low[dx]), device_id_type=MESH)

    @pl.when(owner * near == 1)
    def _():
        for dz in range(1, NZ):
            pl.semaphore_signal(barrier, inc=1, device_id=plane_id(lax.rem(z + dz, NZ)), device_id_type=MESH)

    keep_load.wait()
    top, corner = jnp.zeros((BLOCK, NB), F32), jnp.zeros((BLOCK, BLOCK), F32)
    dims = (((0,), (0,)), ((), ()))
    start = 0
    for i, rows in enumerate(cuts):
        loads[i].wait()
        for at in range(start, start + rows, BLOCK):
            for h in range(NB // BLOCK):
                block = (slice(at, at + BLOCK), slice(h * BLOCK, h * BLOCK + BLOCK))
                masked[block] = jnp.where(keeps[h, at // BLOCK] != 0, masked[block], 0).astype(BF16)
        part = masked[start : start + rows, :]
        top += lax.dot_general(part[:, :BLOCK], part, dims, preferred_element_type=F32)
        corner += lax.dot_general(part[:, BLOCK:], part[:, BLOCK:], dims, preferred_element_type=F32)
        start += rows

    r = lax.broadcasted_iota(jnp.int32, (BLOCK, BLOCK), 0)
    c = lax.broadcasted_iota(jnp.int32, (BLOCK, BLOCK), 1)
    both = jnp.where(c >= r, top[:, :BLOCK], corner)
    diagonal = jnp.sum(jnp.where(c == r, corner, 0.0), axis=0, keepdims=True)
    send[: PIECES // 2, : PIECE - 1, :] = top[:, BLOCK:].reshape(PIECES // 2, PIECE - 1, BLOCK)
    send[PIECES // 2 :, : PIECE - 1, :] = both.reshape(PIECES // 2, PIECE - 1, BLOCK)
    send[:, PIECE - 1 :, :] = jnp.broadcast_to(diagonal[None], (PIECES, 1, BLOCK))

    pl.semaphore_wait(barrier, PIECES + owner * (NEAR - 1 - near))

    def copy(source, target, send_sem, recv_sem, where):
        return pltpu.make_async_remote_copy(
            src_ref=source, dst_ref=target, send_sem=send_sem, recv_sem=recv_sem, device_id=where, device_id_type=MESH)

    def to_owner(n):
        return copy(send.at[n], recv.at[mine], rs_send, rs_recv, spot_id(owner_of(n)))

    def along_z(to):
        return copy(zbuf.at[z], zbuf.at[z], z_send, z_recv, plane_id(to))

    def passed(to):
        return copy(final.at[piece], final.at[piece], pass_send, pass_recv, plane_id(to))

    def gathered(spot):
        return copy(final.at[piece], final.at[piece], ag_send, ag_recv, spot_id(spot))

    def pieces(ref, count, send_sem, recv_sem):
        part = ref.at[pl.ds(0, count)]
        return copy(part, part, send_sem, recv_sem, spot_id((0, 0, 0)))

    for n in PIECE_ORDER:
        pl.when(mine != number(owner_of(n)))(to_owner(n).start)

    @pl.when(owner == 0)
    def _():
        pieces(send, PIECES, rs_send, rs_recv).wait_send()

    @pl.when(owner == 1)
    def _():
        recv[mine] = send[piece]
        pieces(recv, PLANE - 1, rs_send, rs_recv).wait_recv()
        total = recv[0]
        for n in range(1, PLANE):
            total += recv[n]
        zbuf[z] = total
        for to in range(NEAR):
            pl.when(z != to)(along_z(to).start)
        pieces(send, PIECES - 1, rs_send, rs_recv).wait_send()

        @pl.when(near == 1)
        def _():
            pieces(zbuf, NZ - 1, z_send, z_recv).wait_recv()
            total = zbuf[0]
            for n in range(1, NZ):
                total += zbuf[n]
            final[piece] = total

        @pl.when(near == 0)
        def _():
            pieces(final, 1, pass_send, pass_recv).wait_recv()

        for at in range(NEAR):
            if PASSED[at]:
                @pl.when(z == at)
                def _():
                    for to in PASSED[at]:
                        passed(to).start()

        for spot in PLANE_ORDER:
            pl.when(mine != number(spot))(gathered(spot).start)

        @pl.when(near == 1)
        def _():
            pieces(zbuf, NEAR - 1, z_send, z_recv).wait_send()

        @pl.when(near == 0)
        def _():
            pieces(zbuf, NEAR, z_send, z_recv).wait_send()

        for at in range(NEAR):
            if PASSED[at]:
                @pl.when(z == at)
                def _():
                    pieces(final, len(PASSED[at]), pass_send, pass_recv).wait_send()

        pieces(final, PIECES - 1, ag_send, ag_recv).wait_recv()
        pieces(recv, PLANE - 1, ag_send, ag_recv).wait_send()

    @pl.when(owner == 0)
    def _():
        pieces(final, PIECES, ag_send, ag_recv).wait_recv()

    out[...] = final[...]


def summed_gram(matrix, pattern):
    rows = matrix.shape[0]
    cuts = (rows // 4, rows // 4, rows // 2)
    part = (PIECE, BLOCK)
    dma = pltpu.SemaphoreType.DMA
    hbm = pl.BlockSpec(memory_space=pltpu.HBM)
    vmem = pl.BlockSpec(memory_space=pltpu.VMEM)
    return pl.pallas_call(
        functools.partial(gram_kernel, cuts),
        out_shape=(jax.ShapeDtypeStruct((PIECES,) + part, F32), jax.ShapeDtypeStruct((rows, NB), BF16)),
        in_specs=[hbm, hbm],
        out_specs=(vmem, vmem),
        scratch_shapes=[
            pltpu.SMEM(pattern.shape, jnp.int32),
            pltpu.VMEM((PIECES,) + part, F32),
            pltpu.VMEM((PLANE,) + part, F32),
            pltpu.VMEM((NZ,) + part, F32),
            pltpu.VMEM((PIECES,) + part, F32),
            dma((len(cuts),)),
            dma, dma, dma, dma, dma, dma, dma, dma, dma,
        ],
        compiler_params=pltpu.CompilerParams(collective_id=0, has_side_effects=True, vmem_limit_bytes=24 << 20),
        cost_estimate=pl.CostEstimate(flops=2 * rows * NB * NB, bytes_accessed=2 * rows * NB, transcendentals=0),
        name="gram_sum",
    )(matrix, pattern)


def eliminate(panel, at, size, group, tick):
    tiles, lanes = size // 8, panel.shape[1] // 128
    tile = (8, 128)
    parts = [[panel[8 * t : 8 * t + 8, 128 * c : 128 * c + 128] for c in range(lanes)] for t in range(tiles)]
    sub = lax.broadcasted_iota(jnp.int32, tile, 0)
    pivots = [None] * tiles
    for q in range(0, size, group):
        cols = []
        for k in range(q, q + group):
            c, lane = divmod(at + k, 128)
            cols.append([
                jnp.broadcast_to(parts[t][c][:, lane : lane + 1], tile) if t >= k // 8 else None for t in range(tiles)
            ])
        for j in range(q, q + group):
            t0, s = divmod(j, 8)
            col = cols[j - q]
            pivot = jnp.broadcast_to(col[t0][s : s + 1], tile)
            inverse = 1.0 / pivot
            pivots[t0] = pivot if s == 0 else jnp.where(sub >= s, pivot, pivots[t0])
            scaled = [col[t] * inverse if t >= t0 else None for t in range(tiles)]
            for k in range(j + 1, q + group):
                tk, sk = divmod(k, 8)
                row = jnp.broadcast_to(col[tk][sk : sk + 1], tile)
                for t in range(tk, tiles):
                    term = (col[t] * row) * inverse if k == j + 1 else scaled[t] * row
                    cols[k - q][t] = cols[k - q][t] - term
            heads = [jnp.broadcast_to(parts[t0][c][s : s + 1], tile) for c in range(lanes)]
            for t in range(t0, tiles):
                if t == t0 and s == 7:
                    continue
                factors = jnp.where(sub > s, scaled[t], 0.0) if t == t0 else scaled[t]
                for c in range(lanes):
                    parts[t][c] = parts[t][c] - factors * heads[c]
            tick()
    rows = []
    for t in range(tiles):
        scale = lax.rsqrt(pivots[t])
        rows.append(jnp.concatenate([p * scale for p in parts[t]], axis=1))
    return jnp.concatenate(rows, axis=0)


def split(value, terms):
    parts = []
    for _ in range(terms):
        parts.append(value.astype(BF16))
        value = value - parts[-1].astype(F32)
    return parts


def factor(work, size, group, done, tick):
    n = work.shape[0]
    for r0 in range(0, n, size):
        r1 = r0 + size
        low, high = r0 // 128 * 128, n + (r1 + 127) // 128 * 128
        rows = eliminate(work[r0:r1, low:high], r0 - low, size, group, tick)
        work[r0:r1, low:high] = rows
        cut = r1 // 128 * 128
        if r1 < n:
            h, m, l = split(rows, 3)
            left = jnp.concatenate([h, h, m, h, l, m], axis=0)
            right = jnp.concatenate([h, m, h, l, h, m], axis=0)[:, cut - low :]
            for a, e in ((r1, r1 + size), (r1 + size, n)):
                if a < e:
                    work[a:e, cut:high] = work[a:e, cut:high] - lax.dot_general(
                        left[:, a - low : e - low], right, (((0,), (0,)), ((), ())), preferred_element_type=F32)
        done(r1)


def basis_kernel(total_rows, gram, masked, basis, upper, work, triangle, made, out_sems, upper_sem):
    rows = masked.shape[0]
    pieces, chunks = rows // BLOCK, out_sems.shape[1]
    step = rows // chunks

    scale = 1.0 / total_rows
    g01 = gram[: PIECES // 2, : PIECE - 1, :].reshape(BLOCK, BLOCK) * scale
    both = gram[PIECES // 2 :, : PIECE - 1, :].reshape(BLOCK, BLOCK) * scale
    diagonal = gram[0, PIECE - 1 :, :] * scale
    flipped = both.T
    r = lax.broadcasted_iota(jnp.int32, (BLOCK, BLOCK), 0)
    c = lax.broadcasted_iota(jnp.int32, (BLOCK, BLOCK), 1)
    unit = jnp.where(r == c, 1.0, 0.0)
    zero = jnp.zeros((BLOCK, BLOCK), F32)
    work[:BLOCK, :BLOCK] = jnp.where(c >= r, both, flipped)
    work[:BLOCK, BLOCK:NB] = g01
    work[BLOCK:, BLOCK:NB] = jnp.where(c < r, both, jnp.where(c > r, flipped, diagonal))
    work[:BLOCK, NB : NB + BLOCK] = unit
    work[:BLOCK, NB + BLOCK :] = zero
    work[BLOCK:, NB : NB + BLOCK] = zero
    work[BLOCK:, NB + BLOCK :] = unit

    stores = []

    def send_out(i, half):
        part = (pl.ds(i * step, step), pl.ds(half * BLOCK, BLOCK))
        store = pltpu.make_async_copy(made.at[part], basis.at[part], out_sems.at[half, i])
        store.start()
        stores.append(store)

    state = {"weights": None, "ticks": 0, "next": 0}

    def first_half(i):
        rows_i = pl.ds(i * BLOCK, BLOCK)
        left = masked[rows_i, :BLOCK]
        product = jnp.dot(jnp.concatenate([left, left], axis=1), state["weights"], preferred_element_type=F32)
        made[rows_i, :BLOCK] = product.astype(BF16)
        if (i + 1) * BLOCK % step == 0:
            send_out((i + 1) * BLOCK // step - 1, 0)

    def tick():
        if state["weights"] is not None:
            state["ticks"] += 1
            while state["next"] < min(pieces, state["ticks"] * pieces // (NB - BLOCK)):
                first_half(state["next"])
                state["next"] += 1

    def done(count):
        if count == BLOCK:
            corner = jnp.where(c <= r, work[:BLOCK, NB : NB + BLOCK], 0.0).T
            state["weights"] = jnp.concatenate(split(corner, 2), axis=0)

    factor(work, 32, 16, done, tick)

    triangle[:BLOCK, :BLOCK] = jnp.where(c >= r, work[:BLOCK, :BLOCK], 0.0)
    triangle[:BLOCK, BLOCK:] = work[:BLOCK, BLOCK:NB]
    triangle[BLOCK:, :BLOCK] = zero
    triangle[BLOCK:, BLOCK:] = jnp.where(c >= r, work[BLOCK:, BLOCK:NB], 0.0)
    upper_store = pltpu.make_async_copy(triangle, upper, upper_sem)
    upper_store.start()
    stores.append(upper_store)

    corner = jnp.where(c <= r, work[BLOCK:, NB + BLOCK :], 0.0)
    columns = jnp.concatenate([work[BLOCK:, NB : NB + BLOCK].T, corner.T], axis=0)
    weights = jnp.concatenate(split(columns, 2), axis=1)
    for i in range(chunks):
        part = pl.ds(i * step, step)
        product = jnp.dot(masked[part, :], weights, preferred_element_type=F32)
        made[part, BLOCK:] = (product[:, :BLOCK] + product[:, BLOCK:]).astype(BF16)
        send_out(i, 1)
    for store in stores:
        store.wait()


def factor_and_basis(gram, masked, total_rows, chunks=8):
    rows = masked.shape[0]
    vmem = pl.BlockSpec(memory_space=pltpu.VMEM)
    hbm = pl.BlockSpec(memory_space=pltpu.HBM)
    return pl.pallas_call(
        functools.partial(basis_kernel, float(total_rows)),
        out_shape=(jax.ShapeDtypeStruct((rows, NB), BF16), jax.ShapeDtypeStruct((NB, NB), F32)),
        in_specs=[vmem, vmem],
        out_specs=(hbm, hbm),
        scratch_shapes=[
            pltpu.VMEM((NB, 2 * NB), F32),
            pltpu.VMEM((NB, NB), F32),
            pltpu.VMEM((rows, NB), BF16),
            pltpu.SemaphoreType.DMA((2, chunks)),
            pltpu.SemaphoreType.DMA,
        ],
        compiler_params=pltpu.CompilerParams(vmem_limit_bytes=24 << 20),
        cost_estimate=pl.CostEstimate(flops=4 * rows * NB * NB, bytes_accessed=4 * rows * NB, transcendentals=0),
        name="factor_basis",
    )(gram, masked)


def local(matrix, pattern):
    total_rows = matrix.shape[0] * lax.axis_size("gx") * lax.axis_size("gy")
    gram, masked = summed_gram(pltpu.with_memory_space_constraint(matrix, pltpu.HBM), pltpu.with_memory_space_constraint(pattern.T, pltpu.HBM))
    return factor_and_basis(gram, masked, total_rows)


def solution(mesh):
    placed = (P(("gx", "gy"), None), P(("gx", "gy"), None))
    return jax.shard_map(
        local, mesh=mesh, in_specs=placed, out_specs=(P(("gx", "gy"), None), P()), check_vma=False
    )
```

```python
import functools

import jax
import jax.numpy as jnp
from jax import lax
from jax.experimental import pallas as pl
from jax.experimental.pallas import tpu as pltpu
from jax.sharding import PartitionSpec as P

BLOCK = 128
NB = 256
F32 = jnp.float32
BF16 = jnp.bfloat16
MESH = pl.DeviceIdType.MESH

NX, NY, NZ, NC = 4, 4, 16, 2
PLANE = NX * NY * NC
OWNERS = tuple((x, y, 1) for x in range(NX) for y in range(NY))
PIECES = len(OWNERS)
PIECE = NB // PIECES + 1
PASSED = ((), tuple(range(15, 9, -1)), tuple(range(3, 10)))
NEAR = len(PASSED)


def ring(step, size):
    return min(step, size - step)


def sender_order(spot):
    return -(ring(3 - spot[0], NX) + ring(3 - spot[1], NY))


PIECE_ORDER = sorted(range(PIECES), key=lambda n: sender_order(OWNERS[n]))
PLANE_ORDER = sorted(
    ((x, y, core) for x in range(NX) for y in range(NY) for core in range(NC)),
    key=lambda s: (s == (0, 0, 0), s[0] + s[1], s[0], s[1]),
)
PLANE_STEPS = sorted(
    ((dx, dy, dc) for dx in range(NX) for dy in range(NY) for dc in range(NC) if dx or dy or dc),
    key=lambda s: -(ring(s[0], NX) + ring(s[1], NY) + 0.5 * s[2]),
)


def place():
    gx, gy = lax.axis_index("gx"), lax.axis_index("gy")
    x = 2 * lax.div(gx, NY * NC) + lax.div(gy, NZ)
    return x, lax.rem(lax.div(gx, NC), NY), lax.rem(gy, NZ), lax.rem(gx, NC)


def gram_kernel(cuts, matrix, pattern, out, masked, keeps, send, recv, zbuf, final,
                in_sems, keep_sem, rs_send, rs_recv, z_send, z_recv, pass_send, pass_recv, ag_send, ag_recv):
    loads = []
    at = 0
    for i, rows in enumerate(cuts):
        part = pl.ds(at, rows)
        load = pltpu.make_async_copy(matrix.at[part], masked.at[part], in_sems.at[i])
        load.start()
        loads.append(load)
        at += rows
    keep_load = pltpu.make_async_copy(pattern, keeps, keep_sem)
    keep_load.start()

    x, y, z, core = place()
    gx, gy = lax.axis_index("gx"), lax.axis_index("gy")
    mine = (x * NY + y) * NC + core
    owner, piece = 0, 0
    for n, (ox, oy, ocore) in enumerate(OWNERS):
        match = (mine == (ox * NY + oy) * NC + ocore).astype(jnp.int32)
        owner, piece = owner + match, piece + match * n
    near = 1 - lax.div(z + NZ - NEAR, NZ)

    def number(spot):
        return (spot[0] * NY + spot[1]) * NC + spot[2]

    def spot_id(spot):
        return (spot[0] // 2 * NY + spot[1]) * NC + spot[2], spot[0] % 2 * NZ + z

    def plane_id(to):
        return gx, gy - z + to

    barrier = pltpu.get_barrier_semaphore()

    @pl.when(owner == 1)
    def _():
        at_x = [lax.rem(x + d, NX) for d in range(NX)]
        at_y = [lax.rem(y + d, NY) * NC for d in range(NY)]
        at_core = [core, 1 - core]
        high = [lax.div(v, 2) * (NY * NC) for v in at_x]
        low = [lax.rem(v, 2) * NZ + z for v in at_x]
        for dx, dy, dc in PLANE_STEPS:
            pl.semaphore_signal(
                barrier, inc=1, device_id=(high[dx] + at_y[dy] + at_core[dc], low[dx]), device_id_type=MESH)

    @pl.when(owner * near == 1)
    def _():
        for dz in range(1, NZ):
            pl.semaphore_signal(barrier, inc=1, device_id=plane_id(lax.rem(z + dz, NZ)), device_id_type=MESH)

    keep_load.wait()
    top, corner = jnp.zeros((BLOCK, NB), F32), jnp.zeros((BLOCK, BLOCK), F32)
    dims = (((0,), (0,)), ((), ()))
    start = 0
    for i, rows in enumerate(cuts):
        loads[i].wait()
        for at in range(start, start + rows, BLOCK):
            for h in range(NB // BLOCK):
                block = (slice(at, at + BLOCK), slice(h * BLOCK, h * BLOCK + BLOCK))
                masked[block] = jnp.where(keeps[h, at // BLOCK] != 0, masked[block], 0).astype(BF16)
        part = masked[start : start + rows, :]
        top += lax.dot_general(part[:, :BLOCK], part, dims, preferred_element_type=F32)
        corner += lax.dot_general(part[:, BLOCK:], part[:, BLOCK:], dims, preferred_element_type=F32)
        start += rows

    r = lax.broadcasted_iota(jnp.int32, (BLOCK, BLOCK), 0)
    c = lax.broadcasted_iota(jnp.int32, (BLOCK, BLOCK), 1)
    both = jnp.where(c >= r, top[:, :BLOCK], corner)
    diagonal = jnp.sum(jnp.where(c == r, corner, 0.0), axis=0, keepdims=True)
    send[: PIECES // 2, : PIECE - 1, :] = top[:, BLOCK:].reshape(PIECES // 2, PIECE - 1, BLOCK)
    send[PIECES // 2 :, : PIECE - 1, :] = both.reshape(PIECES // 2, PIECE - 1, BLOCK)
    send[:, PIECE - 1 :, :] = jnp.broadcast_to(diagonal[None], (PIECES, 1, BLOCK))

    pl.semaphore_wait(barrier, PIECES + owner * (NEAR - 1 - near))

    def copy(source, target, send_sem, recv_sem, where):
        return pltpu.make_async_remote_copy(
            src_ref=source, dst_ref=target, send_sem=send_sem, recv_sem=recv_sem, device_id=where, device_id_type=MESH)

    def to_owner(n):
        return copy(send.at[n], recv.at[mine], rs_send, rs_recv, spot_id(OWNERS[n]))

    def along_z(to):
        return copy(zbuf.at[z], zbuf.at[z], z_send, z_recv, plane_id(to))

    def passed(to):
        return copy(final.at[piece], final.at[piece], pass_send, pass_recv, plane_id(to))

    def gathered(spot):
        return copy(final.at[piece], final.at[piece], ag_send, ag_recv, spot_id(spot))

    def pieces(ref, count, send_sem, recv_sem):
        part = ref.at[pl.ds(0, count)]
        return copy(part, part, send_sem, recv_sem, spot_id((0, 0, 0)))

    for n in PIECE_ORDER:
        pl.when(mine != number(OWNERS[n]))(to_owner(n).start)

    @pl.when(owner == 0)
    def _():
        pieces(send, PIECES, rs_send, rs_recv).wait_send()

    @pl.when(owner == 1)
    def _():
        recv[mine] = send[piece]
        pieces(recv, PLANE - 1, rs_send, rs_recv).wait_recv()
        total = recv[0]
        for n in range(1, PLANE):
            total += recv[n]
        zbuf[z] = total
        for to in range(NEAR):
            pl.when(z != to)(along_z(to).start)
        pieces(send, PIECES - 1, rs_send, rs_recv).wait_send()

        @pl.when(near == 1)
        def _():
            pieces(zbuf, NZ - 1, z_send, z_recv).wait_recv()
            total = zbuf[0]
            for n in range(1, NZ):
                total += zbuf[n]
            final[piece] = total

        @pl.when(near == 0)
        def _():
            pieces(final, 1, pass_send, pass_recv).wait_recv()

        for at in range(NEAR):
            if PASSED[at]:
                @pl.when(z == at)
                def _():
                    for to in PASSED[at]:
                        passed(to).start()

        for spot in PLANE_ORDER:
            pl.when(mine != number(spot))(gathered(spot).start)

        @pl.when(near == 1)
        def _():
            pieces(zbuf, NEAR - 1, z_send, z_recv).wait_send()

        @pl.when(near == 0)
        def _():
            pieces(zbuf, NEAR, z_send, z_recv).wait_send()

        for at in range(NEAR):
            if PASSED[at]:
                @pl.when(z == at)
                def _():
                    pieces(final, len(PASSED[at]), pass_send, pass_recv).wait_send()

        pieces(final, PIECES - 1, ag_send, ag_recv).wait_recv()
        pieces(recv, PLANE - 1, ag_send, ag_recv).wait_send()

    @pl.when(owner == 0)
    def _():
        pieces(final, PIECES, ag_send, ag_recv).wait_recv()

    out[...] = final[...]


def summed_gram(matrix, pattern):
    rows = matrix.shape[0]
    cuts = (rows // 4, rows // 4, rows // 2)
    part = (PIECE, BLOCK)
    dma = pltpu.SemaphoreType.DMA
    hbm = pl.BlockSpec(memory_space=pltpu.HBM)
    vmem = pl.BlockSpec(memory_space=pltpu.VMEM)
    return pl.pallas_call(
        functools.partial(gram_kernel, cuts),
        out_shape=(jax.ShapeDtypeStruct((PIECES,) + part, F32), jax.ShapeDtypeStruct((rows, NB), BF16)),
        in_specs=[hbm, hbm],
        out_specs=(vmem, vmem),
        scratch_shapes=[
            pltpu.SMEM(pattern.shape, jnp.int32),
            pltpu.VMEM((PIECES,) + part, F32),
            pltpu.VMEM((PLANE,) + part, F32),
            pltpu.VMEM((NZ,) + part, F32),
            pltpu.VMEM((PIECES,) + part, F32),
            dma((len(cuts),)),
            dma, dma, dma, dma, dma, dma, dma, dma, dma,
        ],
        compiler_params=pltpu.CompilerParams(collective_id=0, has_side_effects=True, vmem_limit_bytes=24 << 20),
        cost_estimate=pl.CostEstimate(flops=2 * rows * NB * NB, bytes_accessed=2 * rows * NB, transcendentals=0),
        name="gram_sum",
    )(matrix, pattern)


def eliminate(panel, at, size, group, tick):
    tiles, lanes = size // 8, panel.shape[1] // 128
    tile = (8, 128)
    parts = [[panel[8 * t : 8 * t + 8, 128 * c : 128 * c + 128] for c in range(lanes)] for t in range(tiles)]
    sub = lax.broadcasted_iota(jnp.int32, tile, 0)
    pivots = [None] * tiles
    for q in range(0, size, group):
        cols = []
        for k in range(q, q + group):
            c, lane = divmod(at + k, 128)
            cols.append([
                jnp.broadcast_to(parts[t][c][:, lane : lane + 1], tile) if t >= k // 8 else None for t in range(tiles)
            ])
        for j in range(q, q + group):
            t0, s = divmod(j, 8)
            col = cols[j - q]
            pivot = jnp.broadcast_to(col[t0][s : s + 1], tile)
            inverse = 1.0 / pivot
            pivots[t0] = pivot if s == 0 else jnp.where(sub >= s, pivot, pivots[t0])
            scaled = [col[t] * inverse if t >= t0 else None for t in range(tiles)]
            for k in range(j + 1, q + group):
                tk, sk = divmod(k, 8)
                row = jnp.broadcast_to(col[tk][sk : sk + 1], tile)
                for t in range(tk, tiles):
                    term = (col[t] * row) * inverse if k == j + 1 else scaled[t] * row
                    cols[k - q][t] = cols[k - q][t] - term
            heads = [jnp.broadcast_to(parts[t0][c][s : s + 1], tile) for c in range(lanes)]
            for t in range(t0, tiles):
                if t == t0 and s == 7:
                    continue
                factors = jnp.where(sub > s, scaled[t], 0.0) if t == t0 else scaled[t]
                for c in range(lanes):
                    parts[t][c] = parts[t][c] - factors * heads[c]
            tick()
    rows = []
    for t in range(tiles):
        scale = lax.rsqrt(pivots[t])
        rows.append(jnp.concatenate([p * scale for p in parts[t]], axis=1))
    return jnp.concatenate(rows, axis=0)


def split(value, terms):
    parts = []
    for _ in range(terms):
        parts.append(value.astype(BF16))
        value = value - parts[-1].astype(F32)
    return parts


def factor(work, size, group, done, tick):
    n = work.shape[0]
    for r0 in range(0, n, size):
        r1 = r0 + size
        low, high = r0 // 128 * 128, n + (r1 + 127) // 128 * 128
        rows = eliminate(work[r0:r1, low:high], r0 - low, size, group, tick)
        work[r0:r1, low:high] = rows
        cut = r1 // 128 * 128
        if r1 < n:
            h, m, l = split(rows, 3)
            left = jnp.concatenate([h, h, m, h, l, m], axis=0)
            right = jnp.concatenate([h, m, h, l, h, m], axis=0)[:, cut - low :]
            for a, e in ((r1, r1 + size), (r1 + size, n)):
                if a < e:
                    work[a:e, cut:high] = work[a:e, cut:high] - lax.dot_general(
                        left[:, a - low : e - low], right, (((0,), (0,)), ((), ())), preferred_element_type=F32)
        done(r1)


def basis_kernel(total_rows, gram, masked, basis, upper, work, triangle, made, out_sems, upper_sem):
    rows = masked.shape[0]
    pieces, chunks = rows // BLOCK, out_sems.shape[1]
    step = rows // chunks

    scale = 1.0 / total_rows
    g01 = gram[: PIECES // 2, : PIECE - 1, :].reshape(BLOCK, BLOCK) * scale
    both = gram[PIECES // 2 :, : PIECE - 1, :].reshape(BLOCK, BLOCK) * scale
    diagonal = gram[0, PIECE - 1 :, :] * scale
    flipped = both.T
    r = lax.broadcasted_iota(jnp.int32, (BLOCK, BLOCK), 0)
    c = lax.broadcasted_iota(jnp.int32, (BLOCK, BLOCK), 1)
    unit = jnp.where(r == c, 1.0, 0.0)
    zero = jnp.zeros((BLOCK, BLOCK), F32)
    work[:BLOCK, :BLOCK] = jnp.where(c >= r, both, flipped)
    work[:BLOCK, BLOCK:NB] = g01
    work[BLOCK:, BLOCK:NB] = jnp.where(c < r, both, jnp.where(c > r, flipped, diagonal))
    work[:BLOCK, NB : NB + BLOCK] = unit
    work[:BLOCK, NB + BLOCK :] = zero
    work[BLOCK:, NB : NB + BLOCK] = zero
    work[BLOCK:, NB + BLOCK :] = unit

    stores = []

    def send_out(i, half):
        part = (pl.ds(i * step, step), pl.ds(half * BLOCK, BLOCK))
        store = pltpu.make_async_copy(made.at[part], basis.at[part], out_sems.at[half, i])
        store.start()
        stores.append(store)

    state = {"weights": None, "ticks": 0, "next": 0}

    def first_half(i):
        rows_i = pl.ds(i * BLOCK, BLOCK)
        left = masked[rows_i, :BLOCK]
        product = jnp.dot(jnp.concatenate([left, left], axis=1), state["weights"], preferred_element_type=F32)
        made[rows_i, :BLOCK] = product.astype(BF16)
        if (i + 1) * BLOCK % step == 0:
            send_out((i + 1) * BLOCK // step - 1, 0)

    def tick():
        if state["weights"] is not None:
            state["ticks"] += 1
            while state["next"] < min(pieces, state["ticks"] * pieces // (NB - BLOCK)):
                first_half(state["next"])
                state["next"] += 1

    def done(count):
        if count == BLOCK:
            corner = jnp.where(c <= r, work[:BLOCK, NB : NB + BLOCK], 0.0).T
            state["weights"] = jnp.concatenate(split(corner, 2), axis=0)

    factor(work, 32, 16, done, tick)

    triangle[:BLOCK, :BLOCK] = jnp.where(c >= r, work[:BLOCK, :BLOCK], 0.0)
    triangle[:BLOCK, BLOCK:] = work[:BLOCK, BLOCK:NB]
    triangle[BLOCK:, :BLOCK] = zero
    triangle[BLOCK:, BLOCK:] = jnp.where(c >= r, work[BLOCK:, BLOCK:NB], 0.0)
    upper_store = pltpu.make_async_copy(triangle, upper, upper_sem)
    upper_store.start()
    stores.append(upper_store)

    corner = jnp.where(c <= r, work[BLOCK:, NB + BLOCK :], 0.0)
    columns = jnp.concatenate([work[BLOCK:, NB : NB + BLOCK].T, corner.T], axis=0)
    weights = jnp.concatenate(split(columns, 2), axis=1)
    for i in range(chunks):
        part = pl.ds(i * step, step)
        product = jnp.dot(masked[part, :], weights, preferred_element_type=F32)
        made[part, BLOCK:] = (product[:, :BLOCK] + product[:, BLOCK:]).astype(BF16)
        send_out(i, 1)
    for store in stores:
        store.wait()


def factor_and_basis(gram, masked, total_rows, chunks=8):
    rows = masked.shape[0]
    vmem = pl.BlockSpec(memory_space=pltpu.VMEM)
    hbm = pl.BlockSpec(memory_space=pltpu.HBM)
    return pl.pallas_call(
        functools.partial(basis_kernel, float(total_rows)),
        out_shape=(jax.ShapeDtypeStruct((rows, NB), BF16), jax.ShapeDtypeStruct((NB, NB), F32)),
        in_specs=[vmem, vmem],
        out_specs=(hbm, hbm),
        scratch_shapes=[
            pltpu.VMEM((NB, 2 * NB), F32),
            pltpu.VMEM((NB, NB), F32),
            pltpu.VMEM((rows, NB), BF16),
            pltpu.SemaphoreType.DMA((2, chunks)),
            pltpu.SemaphoreType.DMA,
        ],
        compiler_params=pltpu.CompilerParams(vmem_limit_bytes=24 << 20),
        cost_estimate=pl.CostEstimate(flops=4 * rows * NB * NB, bytes_accessed=4 * rows * NB, transcendentals=0),
        name="factor_basis",
    )(gram, masked)


def local(matrix, pattern):
    total_rows = matrix.shape[0] * lax.axis_size("gx") * lax.axis_size("gy")
    gram, masked = summed_gram(pltpu.with_memory_space_constraint(matrix, pltpu.HBM), pltpu.with_memory_space_constraint(pattern.T, pltpu.HBM))
    return factor_and_basis(gram, masked, total_rows)


def solution(mesh):
    placed = (P(("gx", "gy"), None), P(("gx", "gy"), None))
    return jax.shard_map(
        local, mesh=mesh, in_specs=placed, out_specs=(P(("gx", "gy"), None), P()), check_vma=False
    )
```

```python
import functools

import jax
import jax.numpy as jnp
from jax import lax
from jax.experimental import pallas as pl
from jax.experimental.pallas import tpu as pltpu
from jax.sharding import PartitionSpec as P

BLOCK = 128
NB = 256
F32 = jnp.float32
BF16 = jnp.bfloat16
MESH = pl.DeviceIdType.MESH

NX, NY, NZ, NC = 4, 4, 16, 2
PLANE = NX * NY * NC
OWNERS = tuple(
    (x, y, 1) for x in range(NX) for y in range(NY) if (x, y) not in ((2, 2), (2, 3), (3, 2))
)
PIECES = len(OWNERS)
PIECE = -(-(NB + 1) // PIECES)
PASSED = ((), tuple(range(15, 9, -1)), tuple(range(3, 10)))
NEAR = len(PASSED)


def ring(step, size):
    return min(step, size - step)


def sender_order(spot):
    return -(ring(3 - spot[0], NX) + ring(3 - spot[1], NY))


PIECE_ORDER = sorted(range(PIECES), key=lambda n: sender_order(OWNERS[n]))
FIRST = (0, 0, 1)
PLANE_STEPS = sorted(
    ((dx, dy, dc) for dx in range(NX) for dy in range(NY) for dc in range(NC) if dx or dy or dc),
    key=lambda s: -(ring(s[0], NX) + ring(s[1], NY) + 0.5 * s[2]),
)


def place():
    gx, gy = lax.axis_index("gx"), lax.axis_index("gy")
    x = 2 * lax.div(gx, NY * NC) + lax.div(gy, NZ)
    return x, lax.rem(lax.div(gx, NC), NY), lax.rem(gy, NZ), lax.rem(gx, NC)


def gram_kernel(cuts, matrix, pattern, out, masked, keeps, flat, send, recv, zbuf, final,
                in_sems, keep_sem, rs_send, rs_recv, z_send, z_recv, pass_send, pass_recv, ag_send, ag_recv):
    x, y, z, core = place()
    gx, gy = lax.axis_index("gx"), lax.axis_index("gy")
    mine = (x * NY + y) * NC + core
    owner, piece = 0, 0
    for n, (ox, oy, ocore) in enumerate(OWNERS):
        match = (mine == (ox * NY + oy) * NC + ocore).astype(jnp.int32)
        owner, piece = owner + match, piece + match * n
    near = 1 - lax.div(z + NZ - NEAR, NZ)

    def number(spot):
        return (spot[0] * NY + spot[1]) * NC + spot[2]

    def spot_id(spot):
        return (spot[0] // 2 * NY + spot[1]) * NC + spot[2], spot[0] % 2 * NZ + z

    def plane_id(to):
        return gx, gy - z + to

    barrier = pltpu.get_barrier_semaphore()

    @pl.when(owner == 1)
    def _():
        at_x = [lax.rem(x + d, NX) for d in range(NX)]
        at_y = [lax.rem(y + d, NY) * NC for d in range(NY)]
        at_core = [core, 1 - core]
        high = [lax.div(v, 2) * (NY * NC) for v in at_x]
        low = [lax.rem(v, 2) * NZ + z for v in at_x]
        for dx, dy, dc in PLANE_STEPS:
            pl.semaphore_signal(
                barrier, inc=1, device_id=(high[dx] + at_y[dy] + at_core[dc], low[dx]), device_id_type=MESH)

    @pl.when(owner * near == 1)
    def _():
        for dz in range(1, NZ):
            pl.semaphore_signal(barrier, inc=1, device_id=plane_id(lax.rem(z + dz, NZ)), device_id_type=MESH)

    loads = []
    at = 0
    for i, rows in enumerate(cuts):
        part = pl.ds(at, rows)
        load = pltpu.make_async_copy(matrix.at[part], masked.at[part], in_sems.at[i])
        load.start()
        loads.append(load)
        at += rows
    keep_load = pltpu.make_async_copy(pattern, keeps, keep_sem)
    keep_load.start()

    keep_load.wait()
    top, corner = jnp.zeros((BLOCK, NB), F32), jnp.zeros((BLOCK, BLOCK), F32)
    dims = (((0,), (0,)), ((), ()))
    start = 0
    for i, rows in enumerate(cuts):
        loads[i].wait()
        for at in range(start, start + rows, BLOCK):
            for h in range(NB // BLOCK):
                block = (slice(at, at + BLOCK), slice(h * BLOCK, h * BLOCK + BLOCK))
                masked[block] = jnp.where(keeps[h, at // BLOCK] != 0, masked[block], 0).astype(BF16)
        part = masked[start : start + rows, :]
        top += lax.dot_general(part[:, :BLOCK], part, dims, preferred_element_type=F32)
        corner += lax.dot_general(part[:, BLOCK:], part[:, BLOCK:], dims, preferred_element_type=F32)
        start += rows

    r = lax.broadcasted_iota(jnp.int32, (BLOCK, BLOCK), 0)
    c = lax.broadcasted_iota(jnp.int32, (BLOCK, BLOCK), 1)
    both = jnp.where(c >= r, top[:, :BLOCK], corner)
    diagonal = jnp.sum(jnp.where(c == r, corner, 0.0), axis=0, keepdims=True)
    flat[:BLOCK, :] = top[:, BLOCK:]
    flat[BLOCK:NB, :] = both
    flat[NB:, :] = jnp.broadcast_to(diagonal, (PIECES * PIECE - NB, BLOCK))
    for n in range(PIECES):
        send[n] = flat[n * PIECE : (n + 1) * PIECE, :]

    pl.semaphore_wait(barrier, PIECES + owner * (NEAR - 1 - near))

    def copy(source, target, send_sem, recv_sem, where):
        return pltpu.make_async_remote_copy(
            src_ref=source, dst_ref=target, send_sem=send_sem, recv_sem=recv_sem, device_id=where, device_id_type=MESH)

    def to_owner(n):
        return copy(send.at[n], recv.at[mine], rs_send, rs_recv, spot_id(OWNERS[n]))

    def along_z(to):
        return copy(zbuf.at[z], zbuf.at[z], z_send, z_recv, plane_id(to))

    def passed(to):
        return copy(final.at[piece], final.at[piece], pass_send, pass_recv, plane_id(to))

    def gathered(where):
        return copy(final.at[piece], final.at[piece], ag_send, ag_recv, where)

    def pieces(ref, count, send_sem, recv_sem):
        part = ref.at[pl.ds(0, count)]
        return copy(part, part, send_sem, recv_sem, spot_id((0, 0, 0)))

    for n in PIECE_ORDER:
        pl.when(mine != number(OWNERS[n]))(to_owner(n).start)

    @pl.when(owner == 0)
    def _():
        pieces(send, PIECES, rs_send, rs_recv).wait_send()

    @pl.when(owner == 1)
    def _():
        recv[mine] = send[piece]
        pieces(recv, PLANE - 1, rs_send, rs_recv).wait_recv()
        total = recv[0]
        for n in range(1, PLANE):
            total += recv[n]
        zbuf[z] = total
        for to in range(NEAR):
            pl.when(z != to)(along_z(to).start)
        pieces(send, PIECES - 1, rs_send, rs_recv).wait_send()

        @pl.when(near == 1)
        def _():
            pieces(zbuf, NZ - 1, z_send, z_recv).wait_recv()
            total = zbuf[0]
            for n in range(1, NZ):
                total += zbuf[n]
            final[piece] = total

        @pl.when(near == 0)
        def _():
            pieces(final, 1, pass_send, pass_recv).wait_recv()

        for at in range(NEAR):
            if PASSED[at]:
                @pl.when(z == at)
                def _():
                    for to in PASSED[at]:
                        passed(to).start()

        pl.when(mine != number(FIRST))(gathered(spot_id(FIRST)).start)
        at_x = [lax.rem(x + d, NX) for d in range(NX)]
        at_y = [lax.rem(y + d, NY) for d in range(NY)]
        at_core = [core, 1 - core]
        for dx, dy, dc in PLANE_STEPS:
            to = (at_x[dx], at_y[dy], at_core[dc])
            where = (lax.div(to[0], 2) * NY + to[1]) * NC + to[2], lax.rem(to[0], 2) * NZ + z
            pl.when(number(to) != number(FIRST))(gathered(where).start)

        @pl.when(near == 1)
        def _():
            pieces(zbuf, NEAR - 1, z_send, z_recv).wait_send()

        @pl.when(near == 0)
        def _():
            pieces(zbuf, NEAR, z_send, z_recv).wait_send()

        for at in range(NEAR):
            if PASSED[at]:
                @pl.when(z == at)
                def _():
                    pieces(final, len(PASSED[at]), pass_send, pass_recv).wait_send()

        pieces(final, PIECES - 1, ag_send, ag_recv).wait_recv()
        pieces(recv, PLANE - 1, ag_send, ag_recv).wait_send()

    @pl.when(owner == 0)
    def _():
        pieces(final, PIECES, ag_send, ag_recv).wait_recv()

    for n in range(PIECES):
        out[n * PIECE : (n + 1) * PIECE, :] = final[n]


def summed_gram(matrix, pattern):
    rows = matrix.shape[0]
    cuts = (rows // 4, rows // 4, rows // 2)
    part = (PIECE, BLOCK)
    dma = pltpu.SemaphoreType.DMA
    hbm = pl.BlockSpec(memory_space=pltpu.HBM)
    vmem = pl.BlockSpec(memory_space=pltpu.VMEM)
    return pl.pallas_call(
        functools.partial(gram_kernel, cuts),
        out_shape=(jax.ShapeDtypeStruct((PIECES * PIECE, BLOCK), F32), jax.ShapeDtypeStruct((rows, NB), BF16)),
        in_specs=[hbm, hbm],
        out_specs=(vmem, vmem),
        scratch_shapes=[
            pltpu.SMEM(pattern.shape, jnp.int32),
            pltpu.VMEM((PIECES * PIECE, BLOCK), F32),
            pltpu.VMEM((PIECES,) + part, F32),
            pltpu.VMEM((PLANE,) + part, F32),
            pltpu.VMEM((NZ,) + part, F32),
            pltpu.VMEM((PIECES,) + part, F32),
            dma((len(cuts),)),
            dma, dma, dma, dma, dma, dma, dma, dma, dma,
        ],
        compiler_params=pltpu.CompilerParams(collective_id=0, has_side_effects=True, vmem_limit_bytes=24 << 20),
        cost_estimate=pl.CostEstimate(flops=2 * rows * NB * NB, bytes_accessed=2 * rows * NB, transcendentals=0),
        name="gram_sum",
    )(matrix, pattern)


def eliminate(panel, at, size, group, tick):
    tiles, lanes = size // 8, panel.shape[1] // 128
    tile = (8, 128)
    parts = [[panel[8 * t : 8 * t + 8, 128 * c : 128 * c + 128] for c in range(lanes)] for t in range(tiles)]
    sub = lax.broadcasted_iota(jnp.int32, tile, 0)
    pivots = [None] * tiles
    for q in range(0, size, group):
        cols = []
        for k in range(q, q + group):
            c, lane = divmod(at + k, 128)
            cols.append([
                jnp.broadcast_to(parts[t][c][:, lane : lane + 1], tile) if t >= k // 8 else None for t in range(tiles)
            ])
        for j in range(q, q + group):
            t0, s = divmod(j, 8)
            col = cols[j - q]
            pivot = jnp.broadcast_to(col[t0][s : s + 1], tile)
            inverse = 1.0 / pivot
            pivots[t0] = pivot if s == 0 else jnp.where(sub >= s, pivot, pivots[t0])
            scaled = [col[t] * inverse if t >= t0 else None for t in range(tiles)]
            for k in range(j + 1, q + group):
                tk, sk = divmod(k, 8)
                row = jnp.broadcast_to(col[tk][sk : sk + 1], tile)
                for t in range(tk, tiles):
                    term = (col[t] * row) * inverse if k == j + 1 else scaled[t] * row
                    cols[k - q][t] = cols[k - q][t] - term
            heads = [jnp.broadcast_to(parts[t0][c][s : s + 1], tile) for c in range(lanes)]
            for t in range(t0, tiles):
                if t == t0 and s == 7:
                    continue
                factors = jnp.where(sub > s, scaled[t], 0.0) if t == t0 else scaled[t]
                for c in range(lanes):
                    parts[t][c] = parts[t][c] - factors * heads[c]
            tick()
    rows = []
    for t in range(tiles):
        scale = lax.rsqrt(pivots[t])
        rows.append(jnp.concatenate([p * scale for p in parts[t]], axis=1))
    return jnp.concatenate(rows, axis=0)


def split(value, terms):
    parts = []
    for _ in range(terms):
        parts.append(value.astype(BF16))
        value = value - parts[-1].astype(F32)
    return parts


def factor(work, size, group, done, tick):
    n = work.shape[0]
    for r0 in range(0, n, size):
        r1 = r0 + size
        low, high = r0 // 128 * 128, n + (r1 + 127) // 128 * 128
        rows = eliminate(work[r0:r1, low:high], r0 - low, size, group, tick)
        work[r0:r1, low:high] = rows
        cut = r1 // 128 * 128
        if r1 < n:
            h, m, l = split(rows, 3)
            left = jnp.concatenate([h, h, m, h, l, m], axis=0)
            right = jnp.concatenate([h, m, h, l, h, m], axis=0)[:, cut - low :]
            for a, e in ((r1, r1 + size), (r1 + size, n)):
                if a < e:
                    work[a:e, cut:high] = work[a:e, cut:high] - lax.dot_general(
                        left[:, a - low : e - low], right, (((0,), (0,)), ((), ())), preferred_element_type=F32)
        done(r1)


def basis_kernel(total_rows, gram, masked, basis, upper, work, triangle, made, out_sems, upper_sem):
    rows = masked.shape[0]
    pieces, chunks = rows // BLOCK, out_sems.shape[1]
    step = rows // chunks

    scale = 1.0 / total_rows
    g01 = gram[:BLOCK, :] * scale
    both = gram[BLOCK:NB, :] * scale
    diagonal = gram[NB : NB + 1, :] * scale
    flipped = both.T
    r = lax.broadcasted_iota(jnp.int32, (BLOCK, BLOCK), 0)
    c = lax.broadcasted_iota(jnp.int32, (BLOCK, BLOCK), 1)
    unit = jnp.where(r == c, 1.0, 0.0)
    zero = jnp.zeros((BLOCK, BLOCK), F32)
    work[:BLOCK, :BLOCK] = jnp.where(c >= r, both, flipped)
    work[:BLOCK, BLOCK:NB] = g01
    work[BLOCK:, BLOCK:NB] = jnp.where(c < r, both, jnp.where(c > r, flipped, diagonal))
    work[:BLOCK, NB : NB + BLOCK] = unit
    work[:BLOCK, NB + BLOCK :] = zero
    work[BLOCK:, NB : NB + BLOCK] = zero
    work[BLOCK:, NB + BLOCK :] = unit

    stores = []

    def send_out(i, half):
        part = (pl.ds(i * step, step), pl.ds(half * BLOCK, BLOCK))
        store = pltpu.make_async_copy(made.at[part], basis.at[part], out_sems.at[half, i])
        store.start()
        stores.append(store)

    state = {"weights": None, "ticks": 0, "next": 0}

    def first_half(i):
        rows_i = pl.ds(i * BLOCK, BLOCK)
        left = masked[rows_i, :BLOCK]
        product = jnp.dot(jnp.concatenate([left, left], axis=1), state["weights"], preferred_element_type=F32)
        made[rows_i, :BLOCK] = product.astype(BF16)
        if (i + 1) * BLOCK % step == 0:
            send_out((i + 1) * BLOCK // step - 1, 0)

    def tick():
        if state["weights"] is not None:
            state["ticks"] += 1
            while state["next"] < min(pieces, state["ticks"] * pieces // (NB - BLOCK)):
                first_half(state["next"])
                state["next"] += 1

    def done(count):
        if count == BLOCK:
            corner = jnp.where(c <= r, work[:BLOCK, NB : NB + BLOCK], 0.0).T
            state["weights"] = jnp.concatenate(split(corner, 2), axis=0)

    factor(work, 32, 16, done, tick)

    triangle[:BLOCK, :BLOCK] = jnp.where(c >= r, work[:BLOCK, :BLOCK], 0.0)
    triangle[:BLOCK, BLOCK:] = work[:BLOCK, BLOCK:NB]
    triangle[BLOCK:, :BLOCK] = zero
    triangle[BLOCK:, BLOCK:] = jnp.where(c >= r, work[BLOCK:, BLOCK:NB], 0.0)
    upper_store = pltpu.make_async_copy(triangle, upper, upper_sem)
    upper_store.start()
    stores.append(upper_store)

    corner = jnp.where(c <= r, work[BLOCK:, NB + BLOCK :], 0.0)
    columns = jnp.concatenate([work[BLOCK:, NB : NB + BLOCK].T, corner.T], axis=0)
    weights = jnp.concatenate(split(columns, 2), axis=1)
    for i in range(chunks):
        part = pl.ds(i * step, step)
        product = jnp.dot(masked[part, :], weights, preferred_element_type=F32)
        made[part, BLOCK:] = (product[:, :BLOCK] + product[:, BLOCK:]).astype(BF16)
        send_out(i, 1)
    for store in stores:
        store.wait()


def factor_and_basis(gram, masked, total_rows, chunks=8):
    rows = masked.shape[0]
    vmem = pl.BlockSpec(memory_space=pltpu.VMEM)
    hbm = pl.BlockSpec(memory_space=pltpu.HBM)
    return pl.pallas_call(
        functools.partial(basis_kernel, float(total_rows)),
        out_shape=(jax.ShapeDtypeStruct((rows, NB), BF16), jax.ShapeDtypeStruct((NB, NB), F32)),
        in_specs=[vmem, vmem],
        out_specs=(hbm, hbm),
        scratch_shapes=[
            pltpu.VMEM((NB, 2 * NB), F32),
            pltpu.VMEM((NB, NB), F32),
            pltpu.VMEM((rows, NB), BF16),
            pltpu.SemaphoreType.DMA((2, chunks)),
            pltpu.SemaphoreType.DMA,
        ],
        compiler_params=pltpu.CompilerParams(vmem_limit_bytes=24 << 20),
        cost_estimate=pl.CostEstimate(flops=4 * rows * NB * NB, bytes_accessed=4 * rows * NB, transcendentals=0),
        name="factor_basis",
    )(gram, masked)


def local(matrix, pattern):
    total_rows = matrix.shape[0] * lax.axis_size("gx") * lax.axis_size("gy")
    gram, masked = summed_gram(pltpu.with_memory_space_constraint(matrix, pltpu.HBM), pltpu.with_memory_space_constraint(pattern.T, pltpu.HBM))
    return factor_and_basis(gram, masked, total_rows)


def solution(mesh):
    placed = (P(("gx", "gy"), None), P(("gx", "gy"), None))
    return jax.shard_map(
        local, mesh=mesh, in_specs=placed, out_specs=(P(("gx", "gy"), None), P()), check_vma=False
    )
```

```python
import functools

import jax
import jax.numpy as jnp
from jax import lax
from jax.experimental import pallas as pl
from jax.experimental.pallas import tpu as pltpu
from jax.sharding import PartitionSpec as P

BLOCK = 128
NB = 256
F32 = jnp.float32
BF16 = jnp.bfloat16
MESH = pl.DeviceIdType.MESH

NX, NY, NZ, NC = 4, 4, 16, 2
PLANE = NX * NY * NC
OWNERS = tuple(
    (x, y, 1) for x in range(NX) for y in range(NY) if x < 2 or y < 2
)
PIECES = len(OWNERS)
PIECE = -(-(NB + 1) // PIECES)
PASSED = ((), tuple(range(15, 9, -1)), tuple(range(3, 10)))
NEAR = len(PASSED)


def ring(step, size):
    return min(step, size - step)


def sender_order(spot):
    return -(ring(3 - spot[0], NX) + ring(3 - spot[1], NY))


PIECE_ORDER = sorted(range(PIECES), key=lambda n: sender_order(OWNERS[n]))
FIRST = (0, 0, 1)
PLANE_STEPS = sorted(
    ((dx, dy, dc) for dx in range(NX) for dy in range(NY) for dc in range(NC) if dx or dy or dc),
    key=lambda s: -(ring(s[0], NX) + ring(s[1], NY) + 0.5 * s[2]),
)


def place():
    gx, gy = lax.axis_index("gx"), lax.axis_index("gy")
    x = 2 * lax.div(gx, NY * NC) + lax.div(gy, NZ)
    return x, lax.rem(lax.div(gx, NC), NY), lax.rem(gy, NZ), lax.rem(gx, NC)


def gram_kernel(cuts, matrix, pattern, out, masked, keeps, flat, send, recv, zbuf, final,
                in_sems, keep_sem, rs_send, rs_recv, z_send, z_recv, pass_send, pass_recv, ag_send, ag_recv):
    x, y, z, core = place()
    gx, gy = lax.axis_index("gx"), lax.axis_index("gy")
    mine = (x * NY + y) * NC + core
    owner, piece = 0, 0
    for n, (ox, oy, ocore) in enumerate(OWNERS):
        match = (mine == (ox * NY + oy) * NC + ocore).astype(jnp.int32)
        owner, piece = owner + match, piece + match * n
    near = 1 - lax.div(z + NZ - NEAR, NZ)

    def number(spot):
        return (spot[0] * NY + spot[1]) * NC + spot[2]

    def spot_id(spot):
        return (spot[0] // 2 * NY + spot[1]) * NC + spot[2], spot[0] % 2 * NZ + z

    def plane_id(to):
        return gx, gy - z + to

    barrier = pltpu.get_barrier_semaphore()

    @pl.when(owner == 1)
    def _():
        at_x = [lax.rem(x + d, NX) for d in range(NX)]
        at_y = [lax.rem(y + d, NY) * NC for d in range(NY)]
        at_core = [core, 1 - core]
        high = [lax.div(v, 2) * (NY * NC) for v in at_x]
        low = [lax.rem(v, 2) * NZ + z for v in at_x]
        for dx, dy, dc in PLANE_STEPS:
            pl.semaphore_signal(
                barrier, inc=1, device_id=(high[dx] + at_y[dy] + at_core[dc], low[dx]), device_id_type=MESH)

    @pl.when(owner * near == 1)
    def _():
        for dz in range(1, NZ):
            pl.semaphore_signal(barrier, inc=1, device_id=plane_id(lax.rem(z + dz, NZ)), device_id_type=MESH)

    loads = []
    at = 0
    for i, rows in enumerate(cuts):
        part = pl.ds(at, rows)
        load = pltpu.make_async_copy(matrix.at[part], masked.at[part], in_sems.at[i])
        load.start()
        loads.append(load)
        at += rows
    keep_load = pltpu.make_async_copy(pattern, keeps, keep_sem)
    keep_load.start()

    keep_load.wait()
    top, corner = jnp.zeros((BLOCK, NB), F32), jnp.zeros((BLOCK, BLOCK), F32)
    dims = (((0,), (0,)), ((), ()))
    start = 0
    for i, rows in enumerate(cuts):
        loads[i].wait()
        for at in range(start, start + rows, BLOCK):
            for h in range(NB // BLOCK):
                block = (slice(at, at + BLOCK), slice(h * BLOCK, h * BLOCK + BLOCK))
                masked[block] = jnp.where(keeps[h, at // BLOCK] != 0, masked[block], 0).astype(BF16)
        part = masked[start : start + rows, :]
        top += lax.dot_general(part[:, :BLOCK], part, dims, preferred_element_type=F32)
        corner += lax.dot_general(part[:, BLOCK:], part[:, BLOCK:], dims, preferred_element_type=F32)
        start += rows

    r = lax.broadcasted_iota(jnp.int32, (BLOCK, BLOCK), 0)
    c = lax.broadcasted_iota(jnp.int32, (BLOCK, BLOCK), 1)
    both = jnp.where(c >= r, top[:, :BLOCK], corner)
    diagonal = jnp.sum(jnp.where(c == r, corner, 0.0), axis=0, keepdims=True)
    flat[:BLOCK, :] = top[:, BLOCK:]
    flat[BLOCK:NB, :] = both
    flat[NB:, :] = jnp.broadcast_to(diagonal, (PIECES * PIECE - NB, BLOCK))
    for n in range(PIECES):
        send[n] = flat[n * PIECE : (n + 1) * PIECE, :]

    pl.semaphore_wait(barrier, PIECES + owner * (NEAR - 1 - near))

    def copy(source, target, send_sem, recv_sem, where):
        return pltpu.make_async_remote_copy(
            src_ref=source, dst_ref=target, send_sem=send_sem, recv_sem=recv_sem, device_id=where, device_id_type=MESH)

    def to_owner(n):
        return copy(send.at[n], recv.at[mine], rs_send, rs_recv, spot_id(OWNERS[n]))

    def along_z(to):
        return copy(zbuf.at[z], zbuf.at[z], z_send, z_recv, plane_id(to))

    def passed(to):
        return copy(final.at[piece], final.at[piece], pass_send, pass_recv, plane_id(to))

    def gathered(where):
        return copy(final.at[piece], final.at[piece], ag_send, ag_recv, where)

    def pieces(ref, count, send_sem, recv_sem):
        part = ref.at[pl.ds(0, count)]
        return copy(part, part, send_sem, recv_sem, spot_id((0, 0, 0)))

    for n in PIECE_ORDER:
        pl.when(mine != number(OWNERS[n]))(to_owner(n).start)

    @pl.when(owner == 0)
    def _():
        pieces(send, PIECES, rs_send, rs_recv).wait_send()

    @pl.when(owner == 1)
    def _():
        recv[mine] = send[piece]
        pieces(recv, PLANE - 1, rs_send, rs_recv).wait_recv()
        total = recv[0]
        for n in range(1, PLANE):
            total += recv[n]
        zbuf[z] = total
        for to in range(NEAR):
            pl.when(z != to)(along_z(to).start)
        pieces(send, PIECES - 1, rs_send, rs_recv).wait_send()

        @pl.when(near == 1)
        def _():
            pieces(zbuf, NZ - 1, z_send, z_recv).wait_recv()
            total = zbuf[0]
            for n in range(1, NZ):
                total += zbuf[n]
            final[piece] = total

        @pl.when(near == 0)
        def _():
            pieces(final, 1, pass_send, pass_recv).wait_recv()

        for at in range(NEAR):
            if PASSED[at]:
                @pl.when(z == at)
                def _():
                    for to in PASSED[at]:
                        passed(to).start()

        pl.when(mine != number(FIRST))(gathered(spot_id(FIRST)).start)
        at_x = [lax.rem(x + d, NX) for d in range(NX)]
        at_y = [lax.rem(y + d, NY) for d in range(NY)]
        at_core = [core, 1 - core]
        for dx, dy, dc in PLANE_STEPS:
            to = (at_x[dx], at_y[dy], at_core[dc])
            where = (lax.div(to[0], 2) * NY + to[1]) * NC + to[2], lax.rem(to[0], 2) * NZ + z
            pl.when(number(to) != number(FIRST))(gathered(where).start)

        @pl.when(near == 1)
        def _():
            pieces(zbuf, NEAR - 1, z_send, z_recv).wait_send()

        @pl.when(near == 0)
        def _():
            pieces(zbuf, NEAR, z_send, z_recv).wait_send()

        for at in range(NEAR):
            if PASSED[at]:
                @pl.when(z == at)
                def _():
                    pieces(final, len(PASSED[at]), pass_send, pass_recv).wait_send()

        pieces(final, PIECES - 1, ag_send, ag_recv).wait_recv()
        pieces(recv, PLANE - 1, ag_send, ag_recv).wait_send()

    @pl.when(owner == 0)
    def _():
        pieces(final, PIECES, ag_send, ag_recv).wait_recv()

    for n in range(PIECES):
        out[n * PIECE : (n + 1) * PIECE, :] = final[n]


def summed_gram(matrix, pattern):
    rows = matrix.shape[0]
    cuts = (rows // 4, rows // 4, rows // 2)
    part = (PIECE, BLOCK)
    dma = pltpu.SemaphoreType.DMA
    hbm = pl.BlockSpec(memory_space=pltpu.HBM)
    vmem = pl.BlockSpec(memory_space=pltpu.VMEM)
    return pl.pallas_call(
        functools.partial(gram_kernel, cuts),
        out_shape=(jax.ShapeDtypeStruct((PIECES * PIECE, BLOCK), F32), jax.ShapeDtypeStruct((rows, NB), BF16)),
        in_specs=[hbm, hbm],
        out_specs=(vmem, vmem),
        scratch_shapes=[
            pltpu.SMEM(pattern.shape, jnp.int32),
            pltpu.VMEM((PIECES * PIECE, BLOCK), F32),
            pltpu.VMEM((PIECES,) + part, F32),
            pltpu.VMEM((PLANE,) + part, F32),
            pltpu.VMEM((NZ,) + part, F32),
            pltpu.VMEM((PIECES,) + part, F32),
            dma((len(cuts),)),
            dma, dma, dma, dma, dma, dma, dma, dma, dma,
        ],
        compiler_params=pltpu.CompilerParams(collective_id=0, has_side_effects=True, vmem_limit_bytes=24 << 20),
        cost_estimate=pl.CostEstimate(flops=2 * rows * NB * NB, bytes_accessed=2 * rows * NB, transcendentals=0),
        name="gram_sum",
    )(matrix, pattern)


def eliminate(panel, at, size, group, tick):
    tiles, lanes = size // 8, panel.shape[1] // 128
    tile = (8, 128)
    parts = [[panel[8 * t : 8 * t + 8, 128 * c : 128 * c + 128] for c in range(lanes)] for t in range(tiles)]
    sub = lax.broadcasted_iota(jnp.int32, tile, 0)
    pivots = [None] * tiles
    for q in range(0, size, group):
        cols = []
        for k in range(q, q + group):
            c, lane = divmod(at + k, 128)
            cols.append([
                jnp.broadcast_to(parts[t][c][:, lane : lane + 1], tile) if t >= k // 8 else None for t in range(tiles)
            ])
        for j in range(q, q + group):
            t0, s = divmod(j, 8)
            col = cols[j - q]
            pivot = jnp.broadcast_to(col[t0][s : s + 1], tile)
            inverse = 1.0 / pivot
            pivots[t0] = pivot if s == 0 else jnp.where(sub >= s, pivot, pivots[t0])
            scaled = [col[t] * inverse if t >= t0 else None for t in range(tiles)]
            for k in range(j + 1, q + group):
                tk, sk = divmod(k, 8)
                row = jnp.broadcast_to(col[tk][sk : sk + 1], tile)
                for t in range(tk, tiles):
                    term = (col[t] * row) * inverse if k == j + 1 else scaled[t] * row
                    cols[k - q][t] = cols[k - q][t] - term
            heads = [jnp.broadcast_to(parts[t0][c][s : s + 1], tile) for c in range(lanes)]
            for t in range(t0, tiles):
                if t == t0 and s == 7:
                    continue
                factors = jnp.where(sub > s, scaled[t], 0.0) if t == t0 else scaled[t]
                for c in range(lanes):
                    parts[t][c] = parts[t][c] - factors * heads[c]
            tick()
    rows = []
    for t in range(tiles):
        scale = lax.rsqrt(pivots[t])
        rows.append(jnp.concatenate([p * scale for p in parts[t]], axis=1))
    return jnp.concatenate(rows, axis=0)


def split(value, terms):
    parts = []
    for _ in range(terms):
        parts.append(value.astype(BF16))
        value = value - parts[-1].astype(F32)
    return parts


def factor(work, size, group, done, tick):
    n = work.shape[0]
    for r0 in range(0, n, size):
        r1 = r0 + size
        low, high = r0 // 128 * 128, n + (r1 + 127) // 128 * 128
        rows = eliminate(work[r0:r1, low:high], r0 - low, size, group, tick)
        work[r0:r1, low:high] = rows
        cut = r1 // 128 * 128
        if r1 < n:
            h, m, l = split(rows, 3)
            left = jnp.concatenate([h, h, m, h, l, m], axis=0)
            right = jnp.concatenate([h, m, h, l, h, m], axis=0)[:, cut - low :]
            for a, e in ((r1, r1 + size), (r1 + size, n)):
                if a < e:
                    work[a:e, cut:high] = work[a:e, cut:high] - lax.dot_general(
                        left[:, a - low : e - low], right, (((0,), (0,)), ((), ())), preferred_element_type=F32)
        done(r1)


def basis_kernel(total_rows, gram, masked, basis, upper, work, triangle, made, out_sems, upper_sem):
    rows = masked.shape[0]
    pieces, chunks = rows // BLOCK, out_sems.shape[1]
    step = rows // chunks

    scale = 1.0 / total_rows
    g01 = gram[:BLOCK, :] * scale
    both = gram[BLOCK:NB, :] * scale
    diagonal = gram[NB : NB + 1, :] * scale
    flipped = both.T
    r = lax.broadcasted_iota(jnp.int32, (BLOCK, BLOCK), 0)
    c = lax.broadcasted_iota(jnp.int32, (BLOCK, BLOCK), 1)
    unit = jnp.where(r == c, 1.0, 0.0)
    zero = jnp.zeros((BLOCK, BLOCK), F32)
    work[:BLOCK, :BLOCK] = jnp.where(c >= r, both, flipped)
    work[:BLOCK, BLOCK:NB] = g01
    work[BLOCK:, BLOCK:NB] = jnp.where(c < r, both, jnp.where(c > r, flipped, diagonal))
    work[:BLOCK, NB : NB + BLOCK] = unit
    work[:BLOCK, NB + BLOCK :] = zero
    work[BLOCK:, NB : NB + BLOCK] = zero
    work[BLOCK:, NB + BLOCK :] = unit

    stores = []

    def send_out(i, half):
        part = (pl.ds(i * step, step), pl.ds(half * BLOCK, BLOCK))
        store = pltpu.make_async_copy(made.at[part], basis.at[part], out_sems.at[half, i])
        store.start()
        stores.append(store)

    state = {"weights": None, "ticks": 0, "next": 0}

    def first_half(i):
        rows_i = pl.ds(i * BLOCK, BLOCK)
        left = masked[rows_i, :BLOCK]
        product = jnp.dot(jnp.concatenate([left, left], axis=1), state["weights"], preferred_element_type=F32)
        made[rows_i, :BLOCK] = product.astype(BF16)
        if (i + 1) * BLOCK % step == 0:
            send_out((i + 1) * BLOCK // step - 1, 0)

    def tick():
        if state["weights"] is not None:
            state["ticks"] += 1
            while state["next"] < min(pieces, state["ticks"] * pieces // (NB - BLOCK)):
                first_half(state["next"])
                state["next"] += 1

    def done(count):
        if count == BLOCK:
            corner = jnp.where(c <= r, work[:BLOCK, NB : NB + BLOCK], 0.0).T
            state["weights"] = jnp.concatenate(split(corner, 2), axis=0)

    factor(work, 32, 16, done, tick)

    triangle[:BLOCK, :BLOCK] = jnp.where(c >= r, work[:BLOCK, :BLOCK], 0.0)
    triangle[:BLOCK, BLOCK:] = work[:BLOCK, BLOCK:NB]
    triangle[BLOCK:, :BLOCK] = zero
    triangle[BLOCK:, BLOCK:] = jnp.where(c >= r, work[BLOCK:, BLOCK:NB], 0.0)
    upper_store = pltpu.make_async_copy(triangle, upper, upper_sem)
    upper_store.start()
    stores.append(upper_store)

    corner = jnp.where(c <= r, work[BLOCK:, NB + BLOCK :], 0.0)
    columns = jnp.concatenate([work[BLOCK:, NB : NB + BLOCK].T, corner.T], axis=0)
    weights = jnp.concatenate(split(columns, 2), axis=1)
    for i in range(chunks):
        part = pl.ds(i * step, step)
        product = jnp.dot(masked[part, :], weights, preferred_element_type=F32)
        made[part, BLOCK:] = (product[:, :BLOCK] + product[:, BLOCK:]).astype(BF16)
        send_out(i, 1)
    for store in stores:
        store.wait()


def factor_and_basis(gram, masked, total_rows, chunks=8):
    rows = masked.shape[0]
    vmem = pl.BlockSpec(memory_space=pltpu.VMEM)
    hbm = pl.BlockSpec(memory_space=pltpu.HBM)
    return pl.pallas_call(
        functools.partial(basis_kernel, float(total_rows)),
        out_shape=(jax.ShapeDtypeStruct((rows, NB), BF16), jax.ShapeDtypeStruct((NB, NB), F32)),
        in_specs=[vmem, vmem],
        out_specs=(hbm, hbm),
        scratch_shapes=[
            pltpu.VMEM((NB, 2 * NB), F32),
            pltpu.VMEM((NB, NB), F32),
            pltpu.VMEM((rows, NB), BF16),
            pltpu.SemaphoreType.DMA((2, chunks)),
            pltpu.SemaphoreType.DMA,
        ],
        compiler_params=pltpu.CompilerParams(vmem_limit_bytes=24 << 20),
        cost_estimate=pl.CostEstimate(flops=4 * rows * NB * NB, bytes_accessed=4 * rows * NB, transcendentals=0),
        name="factor_basis",
    )(gram, masked)


def local(matrix, pattern):
    total_rows = matrix.shape[0] * lax.axis_size("gx") * lax.axis_size("gy")
    gram, masked = summed_gram(pltpu.with_memory_space_constraint(matrix, pltpu.HBM), pltpu.with_memory_space_constraint(pattern.T, pltpu.HBM))
    return factor_and_basis(gram, masked, total_rows)


def solution(mesh):
    placed = (P(("gx", "gy"), None), P(("gx", "gy"), None))
    return jax.shard_map(
        local, mesh=mesh, in_specs=placed, out_specs=(P(("gx", "gy"), None), P()), check_vma=False
    )
```
